256 devices in a mesh: users: 16 (over y_hi, z), score: 16 (over y_lo, x, core).
Axes of the slice: x: 4, y: 4 (y_hi: 2, y_lo: 2; y = y_hi * 2 + y_lo), z: 8, core: 2. Of those that a mesh axis runs over, the one named last changes fastest.
Arguments:
- candidates: bfloat16 [32, 6144, 1024], P('users', 'score'), may hold values from -6 to 6
- history: bfloat16 [32, 512, 1024], P('users', 'score'), may hold values from -6 to 6
- proj_weight: bfloat16 [1024, 4, 1024], P(('users', 'score')), may hold values from -0.1875 to 0.1875
- out_weight: bfloat16 [1024, 1024], replicated, may hold values from -0.1875 to 0.1875
- hist_len: int32 [32], P('users'), may hold values from 1 to 512, as said below
- cand_count: int32 [32], P('users'), may hold values from 1 to 6144, as said below
Outputs:
- scored: bfloat16 [32, 6144, 1024], P('users', 'score')
The draws below stay inside these ranges and needn't reach their ends.
Inputs may be any that keep to these rules, and one draw needn't show every extreme that they name: `hist_len`: some user has exactly 512 live events. `cand_count`: some user has exactly 6144 live candidates.
All inputs are finite; a program needn't handle non-finite values.
Results may differ from the reference program's by a relative error of at most 0.0051.
Values may be sent and summed in bfloat16 or wider, within the bound.
A program may use at most 128 MiB of HBM per device.

```python
import math
import jax
import jax.numpy as jnp
from jax import lax

D = 1024
HEADS = 8
USERS = 32
CAND = 6144
HIST = 512


def draw_hist_len(key, part):
    key = jax.random.fold_in(key, 11)
    first_key, second_key = jax.random.split(key)
    lengths = jax.random.randint(first_key, (USERS,), 1, HIST + 1)
    chosen = jax.random.randint(second_key, (), 0, USERS)
    return jnp.where(jnp.arange(USERS) == chosen, HIST, lengths).astype(jnp.int32)


def draw_cand_count(key, part):
    key = jax.random.fold_in(key, 13)
    first_key, second_key = jax.random.split(key)
    counts = jax.random.randint(first_key, (USERS,), 1, CAND + 1)
    chosen = jax.random.randint(second_key, (), 0, USERS)
    return jnp.where(jnp.arange(USERS) == chosen, CAND, counts).astype(jnp.int32)


def steps_of(stream_key, dims, shards, low, high):
    def one(axis_at, shards_of):
        heights = jax.random.uniform(jax.random.fold_in(jax.random.fold_in(stream_key, 6), axis_at), (shards_of,), jnp.float32, low / len(shards), high / len(shards))
        return jnp.repeat(jnp.exp(heights), dims[axis_at] // shards_of).reshape((-1,) + (1,) * (len(dims) - axis_at - 1))

    loudness = one(*shards[0])
    for cut in shards[1:]:
        loudness = loudness * one(*cut)
    return loudness


def gaussian(stream_key, dims, width, bound, cuts=(), kind=jnp.bfloat16):
    gain = steps_of(stream_key, dims, cuts, -0.22, 0.18) if cuts else 1.0
    result = jax.random.normal(stream_key, dims, jnp.float32) * width * gain
    return jnp.minimum(jnp.maximum(result, -bound), bound).astype(kind)


def setup_inputs(seed: int = 0) -> dict:
    key_list = jax.random.split(jax.random.key(seed), 7)
    return {
        "candidates": gaussian(key_list[0], (USERS, CAND, D), 1.0, 6.0, ((0, 16), (1, 16))),
        "history": gaussian(key_list[1], (USERS, HIST, D), 1.0, 6.0, ((0, 16), (1, 16))),
        "proj_weight": gaussian(key_list[2], (D, 4, D), D ** -0.5, 0.1875, ((0, 256),)),
        "out_weight": gaussian(key_list[3], (D, D), D ** -0.5, 0.1875),
        "hist_len": draw_hist_len(jax.random.fold_in(key_list[6], 71), 0),
        "cand_count": draw_cand_count(jax.random.fold_in(key_list[6], 71), 0),
    }


def silu_parts(rows, weight_slab, parts):
    model_width = rows.shape[1]
    flat_weight = weight_slab.reshape(model_width * parts, model_width)
    product = jnp.dot(rows, flat_weight.T, preferred_element_type=jnp.float32)
    shaped = product.reshape(rows.shape[0], model_width, parts)
    return jnp.transpose(jax.nn.silu(shaped), (0, 2, 1)).astype(jnp.bfloat16)

def reference(candidates, history, proj_weight, out_weight, hist_len, cand_count):
    head_size = D // HEADS
    score_scale = 1.0 / math.sqrt(head_size)
    key_value_slab = proj_weight[:, 0:2, :]

    def score_user(user_inputs):
        cand_block, hist_block, hist_limit, cand_limit = user_inputs
        cand_parts = silu_parts(cand_block, proj_weight, 4)
        hist_parts = silu_parts(hist_block, key_value_slab, 2)
        own_key = cand_parts[:, 0].reshape(CAND, HEADS, head_size).astype(jnp.float32)
        own_value = cand_parts[:, 1].reshape(CAND, HEADS, head_size).astype(jnp.float32)
        queries = cand_parts[:, 2].reshape(CAND, HEADS, head_size).astype(jnp.float32)
        user_gate = cand_parts[:, 3].astype(jnp.float32)
        hist_keys = hist_parts[:, 0].reshape(HIST, HEADS, head_size).astype(jnp.float32)
        hist_values = hist_parts[:, 1].reshape(HIST, HEADS, head_size).astype(jnp.float32)
        scores = jnp.einsum('chd,jhd->hcj', queries, hist_keys) * score_scale
        is_live = jnp.arange(HIST, dtype=jnp.int32) < hist_limit
        weights = jnp.where(is_live[None, None, :], jax.nn.silu(scores), 0.0).astype(jnp.bfloat16)
        attended = jnp.einsum('hcj,jhd->chd', weights.astype(jnp.float32), hist_values)
        self_weight = jax.nn.silu(jnp.einsum('chd,chd->ch', queries, own_key) * score_scale)
        attended = attended + self_weight[:, :, None] * own_value
        attn_rows = attended.reshape(CAND, D)
        row_mean = lax.optimization_barrier(jnp.mean(attn_rows, axis=1, keepdims=True))
        centered = attn_rows - row_mean
        row_var = lax.optimization_barrier(jnp.mean(centered * centered, axis=1, keepdims=True))
        normed = centered * lax.rsqrt(row_var + 1e-06)
        gated_rows = (normed * user_gate).astype(jnp.bfloat16)
        mixed_rows = jnp.dot(gated_rows, out_weight, preferred_element_type=jnp.float32) + cand_block.astype(jnp.float32)
        cand_live = jnp.arange(CAND, dtype=jnp.int32) < cand_limit
        return jnp.where(cand_live[:, None], mixed_rows, 0.0).astype(jnp.bfloat16)
    return lax.map(score_user, (candidates, history, hist_len, cand_count))
```

```python
import math

import jax
import jax.numpy as jnp
from jax import lax
from jax.experimental import pallas as pl
from jax.experimental.pallas import tpu as pltpu
from jax.sharding import PartitionSpec as P

MESH = pl.DeviceIdType.MESH
HEADS = 8
NX, NY, NZ = 4, 4, 8
BF16, F32 = jnp.bfloat16, jnp.float32
COLS_X, COLS_Y, COLS_Z = pl.ds(0, 256), pl.ds(256, 384), pl.ds(640, 384)
NSEM = 160


def nt_dot(a, b):
    return lax.dot_general(a, b, (((1,), (1,)), ((), ())), preferred_element_type=F32)


def half_silu(t):
    return t + t * jnp.tanh(t)


def kernel(
    cand_ref, hist_ref, proj_ref, ow_ref, hlen_ref, ccount_ref, out_ref,
    G, H, T, R, cand_v, ow_v, mask_v, attn, gate, gated, out_v, send_sem, recv_sem, local_sem,
):
    u = lax.axis_index("users")
    s = lax.axis_index("score")
    z = lax.rem(u, NZ)
    yhi = lax.div(u, NZ)
    c = lax.rem(s, 2)
    x = lax.rem(lax.div(s, 2), NX)
    ylo = lax.div(s, 8)
    y = yhi * 2 + ylo
    oc = 1 - c

    def dev(px, py, pz, pc):
        return (lax.div(py, 2) * NZ + pz, lax.rem(py, 2) * 8 + px * 2 + pc)

    def up(pos, n, k):
        return lax.rem(pos + k + n, n)

    xo = x + 1 - 2 * lax.rem(x, 2)
    yo = y + 1 - 2 * ylo
    right = {"x": dev(up(x, NX, 1), y, z, c), "y": dev(x, up(y, NY, 1), z, c), "z": dev(x, y, up(z, NZ, 1), c)}
    left = {"x": dev(up(x, NX, -1), y, z, c), "y": dev(x, up(y, NY, -1), z, c), "z": dev(x, y, up(z, NZ, -1), c)}
    sib = dev(x, y, z, oc)
    diag = dev(xo, y, z, oc)

    local = [
        pltpu.make_async_copy(hist_ref, H.at[c, x, ylo], local_sem.at[0]),
        pltpu.make_async_copy(cand_ref, cand_v, local_sem.at[1]),
        pltpu.make_async_copy(ow_ref, ow_v, local_sem.at[2]),
    ]
    for copy in local:
        copy.start()

    barrier = pltpu.get_barrier_semaphore()
    partners = [right["x"], left["x"], right["y"], left["y"], right["z"], left["z"], sib, diag]
    for partner in partners:
        pl.semaphore_signal(barrier, inc=1, device_id=partner, device_id_type=MESH)

    row16 = lax.broadcasted_iota(jnp.int32, (16, 1024), 0)
    for p in range(4):
        tile = jnp.zeros((16, 1024), F32)
        for f in range(4):
            row = proj_ref[f].astype(F32)[p : p + 1]
            tile = jnp.where(row16 == f, jnp.broadcast_to(row, (16, 1024)), tile)
        T[p] = tile.astype(BF16)

    pl.semaphore_wait(barrier, len(partners))

    state = {"k": 0}
    sent = []

    def new_sem():
        k = state["k"]
        state["k"] = k + 1
        return k

    def rcopy(src, dst, k, target):
        return pltpu.make_async_remote_copy(
            src_ref=src, dst_ref=dst, send_sem=send_sem.at[k], recv_sem=recv_sem.at[k],
            device_id=target, device_id_type=MESH,
        )

    def send(src, dst, k, target):
        copy = rcopy(src, dst, k, target)
        copy.start()
        sent.append(copy)

    def wait(dst, k):
        rcopy(dst, dst, k, sib).wait_recv()

    p0 = lax.rem(x, 2) * 2 + c
    xbase = lax.div(x, 2) * 2
    exchange = []
    for step in (1, 2, 3):
        q = lax.rem(p0 + step, 4)
        k = new_sem()
        send(T.at[q], R.at[p0], k, dev(xbase + lax.div(q, 2), y, z, lax.rem(q, 2)))
        exchange.append((k, lax.rem(p0 - step + 4, 4)))
    R[p0] = T[p0]

    k_hist_y = new_sem()
    send(hist_ref, H.at[c, x, ylo], k_hist_y, dev(x, yo, z, c))

    for k, src in exchange:
        wait(R.at[src], k)
    rows = lax.broadcasted_iota(jnp.int32, (16, 64), 0)
    cols = lax.broadcasted_iota(jnp.int32, (16, 64), 1)
    pick = (cols == (rows - (rows & 3)) * 4 + (rows & 3)).astype(F32).astype(BF16)
    received = R[...].reshape(64, 1024)
    slab = lax.dot_general(pick, received, (((1,), (0,)), ((), ())), preferred_element_type=F32)
    G[c, x, y, z] = slab.astype(BF16)

    pos = {"x": x, "y": y, "z": z}
    size = {"x": NX, "y": NY, "z": NZ}
    whole = slice(None)

    def ring(stages, pending):
        for number, (axis, block) in enumerate(stages):
            last = number == len(stages) - 1
            r, n = pos[axis], size[axis]

            def share(at, half):
                if last:
                    k = new_sem()
                    send(block(c, at, half), block(c, at, half), k, sib)
                    pending.append((block(oc, at, half), k))

            got = []
            for j in range(n // 2):
                for at, half, k in got:
                    wait(block(c, at, half), k)
                ends = j == n // 2 - 1
                ahead = []
                for sign, target, half in ((1, right[axis], 0), (-1, left[axis], 1)):
                    half = half if ends else None
                    if ends and half == 1 and block(c, r, 1) is None:
                        continue
                    k = new_sem()
                    mine = up(r, n, -sign * j)
                    send(block(c, mine, half), block(c, mine, half), k, target)
                    ahead.append((up(r, n, -sign * (j + 1)), half, k))
                if j == 0:
                    share(r, None)
                for at, half, k in got:
                    share(at, half)
                got = ahead
                yield
            for at, half, k in got:
                wait(block(c, at, half), k)
                share(at, half)

    def halves(half, n):
        return whole if half is None else pl.ds(half * (n // 2), n // 2)

    def z_first(columns):
        def block(plane, at, half):
            return None if half == 1 else G.at[plane, x, y, at, :, columns]
        return ("z", block)

    color_x = [
        z_first(COLS_X),
        ("y", lambda p, at, h: G.at[p, x, at, halves(h, NZ), :, COLS_X]),
        ("x", lambda p, at, h: G.at[p, at, halves(h, NY), :, :, COLS_X]),
    ]
    color_y = [
        z_first(COLS_Y),
        ("x", lambda p, at, h: G.at[p, at, y, halves(h, NZ), :, COLS_Y]),
        ("y", lambda p, at, h: G.at[p, halves(h, NX), at, :, :, COLS_Y]),
    ]
    color_z = [
        ("x", lambda p, at, h: None if h == 1 else G.at[p, at, y, z, :, COLS_Z]),
        ("y", lambda p, at, h: G.at[p, halves(h, NX), at, z, :, COLS_Z]),
        ("z", lambda p, at, h: G.at[p, halves(h, NX), :, at, :, COLS_Z]),
    ]
    pending = []
    local[0].wait()
    rings = [ring(color_z, pending), ring(color_x, pending), ring(color_y, pending)]
    for run in rings:
        next(run)
    wait(H.at[c, x, 1 - ylo], k_hist_y)
    hist_ring = ring([("x", lambda p, at, h: H.at[p, at] if h is None else H.at[p, at, h])], pending)
    rings.append(hist_ring)
    next(hist_ring)
    for _ in range(12):
        for run in list(rings):
            try:
                next(run)
            except StopIteration:
                rings.remove(run)
    assert not rings
    local[1].wait()
    local[2].wait()
    for view, k in pending:
        wait(view, k)

    head_size = 128
    score_half = 0.5 / math.sqrt(head_size)
    users_here = cand_v.shape[0]

    q = lax.broadcasted_iota(jnp.int32, (512, 128), 0)
    event = (((q >> 5) & 1) * 8 + ((q >> 6) & 3) * 2 + (q >> 8)) * 32 + (q & 31)
    for user in range(users_here):
        mask_v[user] = (event < hlen_ref[user]).astype(F32)

    def head_weight(hi, zp, a, plane):
        return jnp.concatenate(
            [
                G[plane, a + 2 * xp, hi * 2 + yl, pl.ds(2 * zp, 2)].reshape(32, 1024)
                for xp in range(2)
                for yl in range(2)
            ],
            axis=0,
        )

    def one_head(h, carry):
        hi, zp = lax.div(h, 4), lax.rem(h, 4)
        w_kv = jnp.concatenate([head_weight(hi, zp, 0, 0), head_weight(hi, zp, 0, 1)], axis=0)
        w_qg = jnp.concatenate([head_weight(hi, zp, 1, 0), head_weight(hi, zp, 1, 1)], axis=0)
        at = pl.ds(pl.multiple_of(h * 128, 128), 128)
        for user in range(users_here):
            rows_c = cand_v[user]
            rows_h = H[:, :, :, user].reshape(512, 1024)
            kv_h = half_silu(0.5 * nt_dot(rows_h, w_kv))
            keys = kv_h[:, :128].astype(BF16)
            values = (kv_h[:, 128:] * mask_v[user]).astype(BF16)
            qg = half_silu(0.5 * nt_dot(rows_c, w_qg)).astype(BF16)
            kv_c = half_silu(0.5 * nt_dot(rows_c, w_kv)).astype(BF16)
            queries = qg[:, :128]
            gate[user, :, at] = qg[:, 128:]
            weights = half_silu(nt_dot(queries, keys) * score_half).astype(BF16)
            att = lax.dot_general(weights, values, (((1,), (0,)), ((), ())), preferred_element_type=F32)
            own = jnp.sum(queries.astype(F32) * kv_c[:, :128].astype(F32), axis=1, keepdims=True)
            own = half_silu(own * score_half)
            attn[user, :, at] = att + own * kv_c[:, 128:].astype(F32)
        return carry

    lax.fori_loop(0, HEADS, one_head, 0)

    def ow_rows():
        parts = []
        for h in range(HEADS):
            for xp in range(2):
                for yl in range(2):
                    for zl in range(2):
                        first = h * 128 + zl * 64 + yl * 32 + xp * 16
                        parts.append((first, 16))
        return parts

    order = ow_rows()
    slot0 = s * 384
    for user in range(users_here):
        def norm(i, carry):
            block = pl.ds(pl.multiple_of(i * 64, 64), 64)
            rows_a = attn[user, block]
            mean = jnp.sum(rows_a, axis=1, keepdims=True) * (1.0 / 1024)
            centered = rows_a - mean
            var = jnp.sum(centered * centered, axis=1, keepdims=True) * (1.0 / 1024)
            normed = centered * lax.rsqrt(var + 1e-06)
            gated[user, block] = (normed * gate[user, block].astype(F32)).astype(BF16)
            return carry

        lax.fori_loop(0, 6, norm, 0)
        for n in range(4):
            ncols = pl.ds(n * 256, 256)
            ow = jnp.concatenate([ow_v[first : first + size_, n * 256 : n * 256 + 256] for first, size_ in order], axis=0)
            mixed = jnp.dot(gated[user], ow, preferred_element_type=F32)
            mixed = mixed + cand_v[user, :, ncols].astype(F32)
            slot = slot0 + lax.broadcasted_iota(jnp.int32, (384, 256), 0)
            out_v[user, :, ncols] = jnp.where(slot < ccount_ref[user], mixed, 0.0).astype(BF16)
        pltpu.make_async_copy(out_v.at[user], out_ref.at[user], local_sem.at[3 + user]).start()
    for user in range(users_here):
        pltpu.make_async_copy(out_v.at[user], out_ref.at[user], local_sem.at[3 + user]).wait()
    for copy in sent:
        copy.wait_send()
    assert state["k"] <= NSEM


def body(candidates, history, proj_weight, out_weight, hist_len, cand_count):
    anyspace = pl.BlockSpec(memory_space=pl.ANY)
    smem = pl.BlockSpec(memory_space=pltpu.SMEM)
    vmem = pl.BlockSpec(memory_space=pltpu.VMEM)
    return pl.pallas_call(
        kernel,
        out_shape=jax.ShapeDtypeStruct(candidates.shape, BF16),
        in_specs=[anyspace, anyspace, vmem, anyspace, smem, smem],
        out_specs=anyspace,
        scratch_shapes=[
            pltpu.VMEM((2, NX, NY, NZ, 16, 1024), BF16),
            pltpu.VMEM((2, NX, 2, 2, 32, 1024), BF16),
            pltpu.VMEM((4, 16, 1024), BF16),
            pltpu.VMEM((4, 16, 1024), BF16),
            pltpu.VMEM((2, 384, 1024), BF16),
            pltpu.VMEM((1024, 1024), BF16),
            pltpu.VMEM((2, 512, 128), F32),
            pltpu.VMEM((2, 384, 1024), F32),
            pltpu.VMEM((2, 384, 1024), BF16),
            pltpu.VMEM((2, 384, 1024), BF16),
            pltpu.VMEM((2, 384, 1024), BF16),
            pltpu.SemaphoreType.DMA((NSEM,)),
            pltpu.SemaphoreType.DMA((NSEM,)),
            pltpu.SemaphoreType.DMA((5,)),
        ],
        compiler_params=pltpu.CompilerParams(
            collective_id=0, has_side_effects=True, vmem_limit_bytes=56 * 1024 * 1024
        ),
    )(candidates, history, proj_weight, out_weight, hist_len, cand_count)


def solution(mesh):
    in_specs = (
        P("users", "score", None),
        P("users", "score", None),
        P(("users", "score"), None, None),
        P(),
        P("users"),
        P("users"),
    )
    out_specs = P("users", "score", None)
    return jax.shard_map(body, mesh=mesh, in_specs=in_specs, out_specs=out_specs, check_vma=False)
```

```python
import functools
import math

import jax
import jax.numpy as jnp
from jax import lax
from jax.experimental import pallas as pl
from jax.experimental.pallas import tpu as pltpu
from jax.sharding import PartitionSpec as P

MESH = pl.DeviceIdType.MESH
HEADS = 8
NX, NY, NZ = 4, 4, 8
BF16, F32 = jnp.bfloat16, jnp.float32
COLS_X, COLS_Y, COLS_Z = pl.ds(0, 256), pl.ds(256, 384), pl.ds(640, 384)
COLS_XY = pl.ds(0, 640)
SLOT = {0: 0, -1: 1, 1: 2, -2: 3, 2: 4, -3: 5, 3: 6, 4: 7, -4: 7}
NSEM = 128


def nt_dot(a, b):
    return lax.dot_general(a, b, (((1,), (1,)), ((), ())), preferred_element_type=F32)


def half_silu(t):
    return t + t * jnp.tanh(t)


def kernel(
    cand_ref, hist_ref, proj_ref, ow_ref, hlen_ref, ccount_ref, out_ref,
    G, H, T, R, cand_v, ow_v, mask_v, attn, gate, gated, out_v, send_sem, recv_sem, local_sem,
):
    u = lax.axis_index("users")
    s = lax.axis_index("score")
    z = lax.rem(u, NZ)
    yhi = lax.div(u, NZ)
    c = lax.rem(s, 2)
    x = lax.rem(lax.div(s, 2), NX)
    ylo = lax.div(s, 8)
    y = yhi * 2 + ylo
    oc = 1 - c

    def dev(px, py, pz, pc):
        return (lax.div(py, 2) * NZ + pz, lax.rem(py, 2) * 8 + px * 2 + pc)

    def up(pos, n, k):
        return lax.rem(pos + k + n, n)

    xo = x + 1 - 2 * lax.rem(x, 2)
    yo = y + 1 - 2 * ylo
    sib = dev(x, y, z, oc)
    diag = dev(xo, y, z, oc)

    local = [
        pltpu.make_async_copy(hist_ref, H.at[c, x, ylo], local_sem.at[0]),
        pltpu.make_async_copy(cand_ref, cand_v, local_sem.at[1]),
        pltpu.make_async_copy(ow_ref, ow_v, local_sem.at[2]),
    ]
    for copy in local:
        copy.start()

    barrier = pltpu.get_barrier_semaphore()
    partners = [dev(up(x, NX, k), y, z, c) for k in (1, 3, 2)] + [dev(x, up(y, NY, k), z, c) for k in (1, 3, 2)]
    partners += [dev(x, y, up(z, NZ, k), c) for k in (1, 7, 2, 6, 3, 5, 4)] + [sib, diag]
    for partner in partners:
        pl.semaphore_signal(barrier, inc=1, device_id=partner, device_id_type=MESH)

    row16 = lax.broadcasted_iota(jnp.int32, (16, 1024), 0)
    for p in range(4):
        tile = jnp.zeros((16, 1024), F32)
        for f in range(4):
            row = proj_ref[f].astype(F32)[p : p + 1]
            tile = jnp.where(row16 == f, jnp.broadcast_to(row, (16, 1024)), tile)
        T[p] = tile.astype(BF16)

    pl.semaphore_wait(barrier, len(partners))

    state = {"k": 0}
    sent = []

    def new_sem():
        k = state["k"]
        state["k"] = k + 1
        return k

    def rcopy(src, dst, k, target):
        return pltpu.make_async_remote_copy(
            src_ref=src(), dst_ref=dst(), send_sem=send_sem.at[k], recv_sem=recv_sem.at[k],
            device_id=target, device_id_type=MESH,
        )

    def send(src, dst, k, target):
        rcopy(src, dst, k, target).start()
        sent.append((src, k))

    def wait(dst, k):
        rcopy(dst, dst, k, sib).wait_recv()

    p0 = lax.rem(x, 2) * 2 + c
    xbase = lax.div(x, 2) * 2
    exchange = []
    for step in (1, 2, 3):
        q = lax.rem(p0 + step, 4)
        k = new_sem()
        send(functools.partial(T.at.__getitem__, q), lambda: R.at[p0], k, dev(xbase + lax.div(q, 2), y, z, lax.rem(q, 2)))
        exchange.append((k, lax.rem(p0 - step + 4, 4)))
    R[p0] = T[p0]

    k_hist_y = new_sem()
    send(lambda: hist_ref, lambda: H.at[c, x, ylo], k_hist_y, dev(x, yo, z, c))

    for k, src in exchange:
        wait(functools.partial(R.at.__getitem__, src), k)
    rows = lax.broadcasted_iota(jnp.int32, (16, 64), 0)
    cols = lax.broadcasted_iota(jnp.int32, (16, 64), 1)
    pick = (cols == (rows - (rows & 3)) * 4 + (rows & 3)).astype(F32).astype(BF16)
    received = R[...].reshape(64, 1024)
    slab = lax.dot_general(pick, received, (((1,), (0,)), ((), ())), preferred_element_type=F32)
    G[c, x, y, 0] = slab.astype(BF16)

    whole = slice(None)

    def view(plane, xs, ys, slots, columns):
        return lambda: G.at[plane, xs, ys, slots, :, columns]

    def direct(axis, block):
        n, at = (NX, x) if axis == "x" else (NY, y)
        arrivals = []
        for step in (1, 3, 2):
            k = new_sem()
            to = up(at, n, step)
            send(block(at), block(at), k, dev(to, y, z, c) if axis == "x" else dev(x, to, z, c))
            arrivals.append((block(up(at, n, -step)), k))
        return arrivals

    def settle(arrivals):
        for where, k in arrivals:
            wait(where, k)

    waves = [pl.ds(0, 1), pl.ds(1, 2), pl.ds(3, 2), pl.ds(5, 2), pl.ds(7, 1)]

    def second(w):
        group_x = direct("y", lambda at: view(c, x, at, waves[w], COLS_X))
        group_y = direct("x", lambda at: view(c, at, y, waves[w], COLS_Y))
        return group_x, group_y

    def third(w, arrivals):
        settle(arrivals[0])
        group_x = direct("x", lambda at: view(c, at, whole, waves[w], COLS_X))
        settle(arrivals[1])
        group_y = direct("y", lambda at: view(c, whole, at, waves[w], COLS_Y))
        return group_x + group_y

    zx = direct("x", lambda at: view(c, at, y, 0, COLS_Z))
    along_z = {}
    for off in (1, -1, 2, -2, 3, -3, 4):
        k = new_sem()
        send(view(c, x, y, 0, COLS_XY), view(c, x, y, SLOT[-off], COLS_XY), k, dev(x, y, up(z, NZ, off), c))
        along_z[SLOT[-off]] = (view(c, x, y, SLOT[-off], COLS_XY), k)
    stage2 = {0: second(0)}
    settle(zx)
    zy = direct("y", lambda at: view(c, whole, at, 0, COLS_Z))
    stage3 = {0: third(0, stage2[0])}
    local[0].wait()
    wait(lambda: H.at[c, x, 1 - ylo], k_hist_y)
    settle([along_z[1], along_z[2]])
    stage2[1] = second(1)
    hist_x = direct("x", lambda at: lambda: H.at[c, at])
    settle(zy)

    z_right, z_left = dev(x, y, up(z, NZ, 1), c), dev(x, y, up(z, NZ, -1), c)
    ring_sems = [(new_sem(), new_sem()) for _ in range(4)]
    twin_sems = [new_sem() for _ in range(6)]

    def ring_blocks(w):
        xs = (whole, whole) if w < 4 else (pl.ds(0, 2), pl.ds(2, 2))
        down, high = (2 * w - 3, 2 * w - 2) if w > 1 else (0, 0)
        into = (2 * w - 1, 2 * w) if w < 4 else (7, 7)
        return [
            (view(c, xs[0], whole, down, COLS_Z), view(c, xs[0], whole, into[0], COLS_Z)),
            (view(c, xs[1], whole, high, COLS_Z), view(c, xs[1], whole, into[1], COLS_Z)),
        ]

    def ring_send(w):
        for (src, dst), k, target in zip(ring_blocks(w), ring_sems[w - 1], (z_right, z_left)):
            send(src, dst, k, target)

    def ring_wait(w):
        for (_, dst), k in zip(ring_blocks(w), ring_sems[w - 1]):
            wait(dst, k)

    def twin_send(w):
        block = view(c, whole, whole, waves[w], whole)
        send(block, block, twin_sems[w], sib)

    def twin_wait(w):
        wait(view(oc, whole, whole, waves[w], whole), twin_sems[w])

    ring_send(1)
    stage3[1] = third(1, stage2[1])
    settle([along_z[3], along_z[4]])
    stage2[2] = second(2)
    settle([along_z[5], along_z[6], along_z[7]])
    stage2[3] = second(3)
    stage2[4] = second(4)
    settle(stage3[0])
    twin_send(0)
    stage3[2] = third(2, stage2[2])
    settle(hist_x)
    send(lambda: H.at[c], lambda: H.at[c], twin_sems[5], sib)
    stage3[3] = third(3, stage2[3])
    stage3[4] = third(4, stage2[4])
    local[1].wait()
    local[2].wait()
    ring_wait(1)
    ring_send(2)
    settle(stage3[1])
    twin_send(1)
    wait(lambda: H.at[oc], twin_sems[5])
    twin_wait(0)
    twin_wait(1)

    head_size = 128
    score_half = 0.5 / math.sqrt(head_size)
    users_here = cand_v.shape[0]

    q = lax.broadcasted_iota(jnp.int32, (512, 128), 0)
    event = (((q >> 5) & 1) * 8 + ((q >> 6) & 3) * 2 + (q >> 8)) * 32 + (q & 31)
    for user in range(users_here):
        mask_v[user] = (event < hlen_ref[user]).astype(F32)

    odd = lax.rem(z, 2)

    def head_weight(hi, slots, a, plane):
        return jnp.concatenate(
            [G[plane, a + 2 * xp, hi * 2 + yl, slot] for xp in range(2) for yl in range(2) for slot in slots],
            axis=0,
        )

    def choose(t, even_slots, odd_slots):
        slot = jnp.int32(0)
        for number in range(4):
            slot = jnp.where(t == number, jnp.where(odd == 1, odd_slots[number], even_slots[number]), slot)
        return slot

    def one_head(i, carry):
        for w in (2, 3, 4):
            @pl.when(i == 2 * w - 3)
            def _():
                ring_wait(w)
                if w < 4:
                    ring_send(w + 1)
                settle(stage3[w])
                twin_send(w)

            @pl.when(i == 2 * w - 2)
            def _():
                twin_wait(w)

        t, hi = lax.div(i, 2), lax.rem(i, 2)
        turn = t + lax.div(t, 2) - 2 * lax.div(t, 3)
        h = hi * 4 + lax.rem(lax.div(z, 2) + (2 * odd - 1) * turn + 8, 4)
        slots = (choose(t, (0, 3, 4, 7), (1, 2, 5, 6)), choose(t, (2, 1, 6, 5), (0, 4, 3, 7)))
        w_kv = jnp.concatenate([head_weight(hi, slots, 0, 0), head_weight(hi, slots, 0, 1)], axis=0)
        w_qg = jnp.concatenate([head_weight(hi, slots, 1, 0), head_weight(hi, slots, 1, 1)], axis=0)
        at = pl.ds(pl.multiple_of(h * 128, 128), 128)
        for user in range(users_here):
            rows_c = cand_v[user]
            rows_h = H[:, :, :, user].reshape(512, 1024)
            kv_h = half_silu(0.5 * nt_dot(rows_h, w_kv))
            keys = kv_h[:, :128].astype(BF16)
            values = (kv_h[:, 128:] * mask_v[user]).astype(BF16)
            qg = half_silu(0.5 * nt_dot(rows_c, w_qg)).astype(BF16)
            kv_c = half_silu(0.5 * nt_dot(rows_c, w_kv)).astype(BF16)
            queries = qg[:, :128]
            gate[user, :, at] = qg[:, 128:]
            weights = half_silu(nt_dot(queries, keys) * score_half).astype(BF16)
            att = lax.dot_general(weights, values, (((1,), (0,)), ((), ())), preferred_element_type=F32)
            own = jnp.sum(queries.astype(F32) * kv_c[:, :128].astype(F32), axis=1, keepdims=True)
            own = half_silu(own * score_half)
            attn[user, :, at] = att + own * kv_c[:, 128:].astype(F32)
        return carry

    lax.fori_loop(0, HEADS, one_head, 0)

    def ow_rows():
        parts = []
        for h in range(HEADS):
            for xp in range(2):
                for yl in range(2):
                    for zl in range(2):
                        first = h * 128 + zl * 64 + yl * 32 + xp * 16
                        parts.append((first, 16))
        return parts

    order = ow_rows()
    slot0 = s * 384
    for user in range(users_here):
        def norm(i, carry):
            block = pl.ds(pl.multiple_of(i * 64, 64), 64)
            rows_a = attn[user, block]
            mean = jnp.sum(rows_a, axis=1, keepdims=True) * (1.0 / 1024)
            centered = rows_a - mean
            var = jnp.sum(centered * centered, axis=1, keepdims=True) * (1.0 / 1024)
            normed = centered * lax.rsqrt(var + 1e-06)
            gated[user, block] = (normed * gate[user, block].astype(F32)).astype(BF16)
            return carry

        lax.fori_loop(0, 6, norm, 0)
        for n in range(4):
            ncols = pl.ds(n * 256, 256)
            ow = jnp.concatenate([ow_v[first : first + size_, n * 256 : n * 256 + 256] for first, size_ in order], axis=0)
            mixed = jnp.dot(gated[user], ow, preferred_element_type=F32)
            mixed = mixed + cand_v[user, :, ncols].astype(F32)
            slot = slot0 + lax.broadcasted_iota(jnp.int32, (384, 256), 0)
            out_v[user, :, ncols] = jnp.where(slot < ccount_ref[user], mixed, 0.0).astype(BF16)
        pltpu.make_async_copy(out_v.at[user], out_ref.at[user], local_sem.at[3 + user]).start()
    for user in range(users_here):
        pltpu.make_async_copy(out_v.at[user], out_ref.at[user], local_sem.at[3 + user]).wait()
    for src, k in sent:
        rcopy(src, src, k, sib).wait_send()
    assert state["k"] <= NSEM


def body(candidates, history, proj_weight, out_weight, hist_len, cand_count):
    anyspace = pl.BlockSpec(memory_space=pl.ANY)
    smem = pl.BlockSpec(memory_space=pltpu.SMEM)
    vmem = pl.BlockSpec(memory_space=pltpu.VMEM)
    return pl.pallas_call(
        kernel,
        out_shape=jax.ShapeDtypeStruct(candidates.shape, BF16),
        in_specs=[anyspace, anyspace, vmem, anyspace, smem, smem],
        out_specs=anyspace,
        scratch_shapes=[
            pltpu.VMEM((2, NX, NY, NZ, 16, 1024), BF16),
            pltpu.VMEM((2, NX, 2, 2, 32, 1024), BF16),
            pltpu.VMEM((4, 16, 1024), BF16),
            pltpu.VMEM((4, 16, 1024), BF16),
            pltpu.VMEM((2, 384, 1024), BF16),
            pltpu.VMEM((1024, 1024), BF16),
            pltpu.VMEM((2, 512, 128), F32),
            pltpu.VMEM((2, 384, 1024), F32),
            pltpu.VMEM((2, 384, 1024), BF16),
            pltpu.VMEM((2, 384, 1024), BF16),
            pltpu.VMEM((2, 384, 1024), BF16),
            pltpu.SemaphoreType.DMA((NSEM,)),
            pltpu.SemaphoreType.DMA((NSEM,)),
            pltpu.SemaphoreType.DMA((5,)),
        ],
        compiler_params=pltpu.CompilerParams(
            collective_id=0, has_side_effects=True, vmem_limit_bytes=56 * 1024 * 1024
        ),
    )(candidates, history, proj_weight, out_weight, hist_len, cand_count)


def solution(mesh):
    in_specs = (
        P("users", "score", None),
        P("users", "score", None),
        P(("users", "score"), None, None),
        P(),
        P("users"),
        P("users"),
    )
    out_specs = P("users", "score", None)
    return jax.shard_map(body, mesh=mesh, in_specs=in_specs, out_specs=out_specs, check_vma=False)
```

```python
import math

import jax
import jax.numpy as jnp
from jax import lax
from jax.experimental import pallas as pl
from jax.experimental.pallas import tpu as pltpu
from jax.sharding import PartitionSpec as P

MESH = pl.DeviceIdType.MESH
HEADS = 8
NX, NY, NZ = 4, 4, 8
BF16, F32 = jnp.bfloat16, jnp.float32
COLS_X, COLS_Y, COLS_Z = pl.ds(0, 256), pl.ds(256, 384), pl.ds(640, 384)
COLS_XY = pl.ds(0, 640)
SLOT = {0: 0, -1: 1, 1: 2, -2: 3, 2: 4, -3: 5, 3: 6, 4: 7, -4: 7}
NSEM = 128


def nt_dot(a, b):
    return lax.dot_general(a, b, (((1,), (1,)), ((), ())), preferred_element_type=F32)


def half_silu(t):
    return t + t * jnp.tanh(t)


def kernel(
    cand_ref, hist_ref, proj_ref, ow_ref, hlen_ref, ccount_ref, out_ref,
    G, H, KV, W, pick_v, cand_v, ow_v, mask_v, attn, gate, gated, out_v, send_sem, recv_sem, local_sem,
):
    u = lax.axis_index("users")
    s = lax.axis_index("score")
    z = lax.rem(u, NZ)
    yhi = lax.div(u, NZ)
    c = lax.rem(s, 2)
    x = lax.rem(lax.div(s, 2), NX)
    ylo = lax.div(s, 8)
    y = yhi * 2 + ylo
    oc = 1 - c

    def dev(px, py, pz, pc):
        return (lax.div(py, 2) * NZ + pz, lax.rem(py, 2) * 8 + px * 2 + pc)

    def up(pos, n, k):
        return lax.rem(pos + k + n, n)

    yo = y + 1 - 2 * ylo
    sib = dev(x, y, z, oc)
    local = [
        pltpu.make_async_copy(hist_ref.at[c], H.at[x, ylo, c], local_sem.at[0]),
        pltpu.make_async_copy(cand_ref, cand_v, local_sem.at[1]),
        pltpu.make_async_copy(ow_ref, ow_v, local_sem.at[2]),
    ]
    for copy in local:
        copy.start()

    barrier = pltpu.get_barrier_semaphore()
    partners = [dev(up(x, NX, k), y, z, c) for k in (1, 3, 2)] + [dev(x, up(y, NY, k), z, c) for k in (1, 3, 2)]
    partners += [dev(x, y, up(z, NZ, k), c) for k in (1, 7, 2, 6, 3, 5, 4)] + [sib]
    for partner in partners:
        pl.semaphore_signal(barrier, inc=1, device_id=partner, device_id_type=MESH)

    row16 = lax.broadcasted_iota(jnp.int32, (16, 1024), 0)
    tile = jnp.zeros((16, 1024), F32)
    for f in range(4):
        rows_f = proj_ref[f].astype(F32)
        for p in range(4):
            tile = jnp.where(row16 == f * 4 + p, jnp.broadcast_to(rows_f[p : p + 1], (16, 1024)), tile)
    G[c, x, y, 0] = tile.astype(BF16)

    pl.semaphore_wait(barrier, len(partners))

    state = {"k": 0}
    sent = []

    def new_sem():
        k = state["k"]
        state["k"] = k + 1
        return k

    def rcopy(src, dst, k, target):
        return pltpu.make_async_remote_copy(
            src_ref=src(), dst_ref=dst(), send_sem=send_sem.at[k], recv_sem=recv_sem.at[k],
            device_id=target, device_id_type=MESH,
        )

    def send(src, dst, k, target):
        rcopy(src, dst, k, target).start()
        sent.append((src, k))

    def wait(dst, k):
        rcopy(dst, dst, k, sib).wait_recv()

    k_hist_c = new_sem()
    send(lambda: hist_ref.at[oc], lambda: H.at[x, ylo, c], k_hist_c, sib)

    whole = slice(None)

    def view(plane, xs, ys, slots, columns):
        return lambda: G.at[plane, xs, ys, slots, :, columns]

    def direct(axis, block):
        n, at = (NX, x) if axis == "x" else (NY, y)
        arrivals = []
        for step in (1, 3, 2):
            k = new_sem()
            to = up(at, n, step)
            send(block(at), block(at), k, dev(to, y, z, c) if axis == "x" else dev(x, to, z, c))
            arrivals.append((block(up(at, n, -step)), k))
        return arrivals

    def settle(arrivals):
        for where, k in arrivals:
            wait(where, k)

    waves = [pl.ds(0, 1), pl.ds(1, 2), pl.ds(3, 2), pl.ds(5, 2), pl.ds(7, 1)]

    def second(w):
        group_x = direct("y", lambda at: view(c, x, at, waves[w], COLS_X))
        group_y = direct("x", lambda at: view(c, at, y, waves[w], COLS_Y))
        return group_x, group_y

    def third(w, arrivals):
        settle(arrivals[0])
        group_x = direct("x", lambda at: view(c, at, whole, waves[w], COLS_X))
        settle(arrivals[1])
        group_y = direct("y", lambda at: view(c, whole, at, waves[w], COLS_Y))
        return group_x + group_y

    spot = {"x": [up(x, NX, k) for k in range(NX)], "y": [up(y, NY, k) for k in range(NY)]}
    neighbour = {
        "x": [dev(spot["x"][k], y, z, c) for k in range(NX)],
        "y": [dev(x, spot["y"][k], z, c) for k in range(NY)],
    }

    def ring_first(axis, block):
        arrivals = []
        for step in (1, 3):
            k = new_sem()
            send(block(spot[axis][0], None), block(spot[axis][0], None), k, neighbour[axis][step])
            arrivals.append((block(spot[axis][4 - step], None), k))
        sems = [new_sem(), new_sem()]
        return arrivals, sems, [(block(spot[axis][2], half), sems[half]) for half in range(2)]

    def ring_second(axis, block, started):
        settle(started[0])
        for half, step in ((0, 1), (1, 3)):
            mine = block(spot[axis][4 - step], half)
            send(mine, mine, started[1][half], neighbour[axis][step])
        return started[2]

    def part(half):
        return whole if half is None else pl.ds(2 * half, 2)

    def wave_x(w):
        return "x", lambda at, half: view(c, at, part(half), waves[w], COLS_X)

    def wave_y(w):
        return "y", lambda at, half: view(c, part(half), at, waves[w], COLS_Y)

    def third_first(w, arrivals):
        settle(arrivals[0])
        group_x = ring_first(*wave_x(w))
        settle(arrivals[1])
        group_y = ring_first(*wave_y(w))
        return group_x, group_y

    def third_second(w):
        ring_second(*wave_x(w), stage3[w][0])
        ring_second(*wave_y(w), stage3[w][1])

    def hist_block(at, half):
        return (lambda: H.at[at]) if half is None else (lambda: H.at[at, half])

    zx = direct("x", lambda at: view(c, at, y, 0, COLS_Z))
    along_z = {}
    for off in (1, -1, 2, -2, 3, -3, 4):
        k = new_sem()
        send(view(c, x, y, 0, COLS_XY), view(c, x, y, SLOT[-off], COLS_XY), k, dev(x, y, up(z, NZ, off), c))
        along_z[SLOT[-off]] = (view(c, x, y, SLOT[-off], COLS_XY), k)
    stage2 = {0: second(0)}
    local[0].wait()
    wait(lambda: H.at[x, ylo, oc], k_hist_c)
    k_hist_y = new_sem()
    send(lambda: H.at[x, ylo], lambda: H.at[x, ylo], k_hist_y, dev(x, yo, z, c))
    settle(zx)
    zy = direct("y", lambda at: view(c, whole, at, 0, COLS_Z))
    stage3 = {0: third(0, stage2[0])}
    wait(lambda: H.at[x, 1 - ylo], k_hist_y)
    hist_x = ring_first("x", hist_block)
    settle([along_z[1], along_z[2]])
    stage2[1] = second(1)
    settle(zy)

    z_right, z_left = dev(x, y, up(z, NZ, 1), c), dev(x, y, up(z, NZ, -1), c)
    ring_sems = [(new_sem(), new_sem()) for _ in range(4)]
    twin_sems = [new_sem() for _ in range(5)]
    kv_sems = [new_sem() for _ in range(HEADS)]

    def ring_blocks(w):
        xs = (whole, whole) if w < 4 else (pl.ds(0, 2), pl.ds(2, 2))
        down, high = (2 * w - 3, 2 * w - 2) if w > 1 else (0, 0)
        into = (2 * w - 1, 2 * w) if w < 4 else (7, 7)
        return [
            (view(c, xs[0], whole, down, COLS_Z), view(c, xs[0], whole, into[0], COLS_Z)),
            (view(c, xs[1], whole, high, COLS_Z), view(c, xs[1], whole, into[1], COLS_Z)),
        ]

    def ring_send(w):
        for (src, dst), k, target in zip(ring_blocks(w), ring_sems[w - 1], (z_right, z_left)):
            send(src, dst, k, target)

    def ring_wait(w):
        for (_, dst), k in zip(ring_blocks(w), ring_sems[w - 1]):
            wait(dst, k)

    def twin_send(w):
        block = view(c, whole, whole, waves[w], whole)
        send(block, block, twin_sems[w], sib)

    def twin_wait(w):
        wait(view(oc, whole, whole, waves[w], whole), twin_sems[w])

    ring_send(1)
    stage3[1] = third(1, stage2[1])
    settle([along_z[3], along_z[4]])
    stage2[2] = second(2)
    hist_x = ring_second("x", hist_block, hist_x)
    settle([along_z[5], along_z[6], along_z[7]])
    stage2[3] = second(3)
    stage2[4] = second(4)
    settle(stage3[0])
    twin_send(0)
    stage3[2] = third_first(2, stage2[2])
    stage3[3] = third_first(3, stage2[3])
    stage3[4] = third_first(4, stage2[4])
    local[1].wait()
    local[2].wait()
    ring_wait(1)
    ring_send(2)
    settle(stage3[1])
    twin_send(1)
    third_second(2)
    settle(hist_x)
    twin_wait(0)
    twin_wait(1)

    head_size = 128
    score_half = 0.5 / math.sqrt(head_size)
    users_here = cand_v.shape[0]

    q = lax.broadcasted_iota(jnp.int32, (512, 128), 0)
    event = (((q >> 6) & 1) * 8 + (q >> 7) * 2 + ((q >> 5) & 1)) * 32 + (q & 31)
    mask_v[...] = (event < hlen_ref[c]).astype(F32)
    out_row = lax.broadcasted_iota(jnp.int32, (256, 256), 0)
    in_row = lax.broadcasted_iota(jnp.int32, (256, 256), 1)
    source = ((out_row & 63) >> 2) * 16 + (out_row & 3) * 4 + (out_row >> 6)
    pick_v[...] = (in_row == source).astype(F32).astype(BF16)

    odd = lax.rem(z, 2)

    def slabs(hi, slot):
        return jnp.concatenate(
            [G[plane, px, hi * 2 + yl, slot] for yl in range(2) for px in range(NX) for plane in range(2)],
            axis=0,
        )

    def choose(t, even_slots, odd_slots):
        slot = jnp.int32(0)
        for number in range(4):
            slot = jnp.where(t == number, jnp.where(odd == 1, odd_slots[number], even_slots[number]), slot)
        return slot

    def chunk(t, carry):
        for w in (2, 3, 4):
            @pl.when(t == w - 1)
            def _():
                twin_wait(w)

        turn = t + lax.div(t, 2) - 2 * lax.div(t, 3)
        pair = lax.rem(lax.div(z, 2) + (2 * odd - 1) * turn + 8, 4)
        slots = (choose(t, (0, 3, 4, 7), (1, 2, 5, 6)), choose(t, (2, 1, 6, 5), (0, 4, 3, 7)))

        def keys_values(hi, carry):
            for zl in range(2):
                sorted_rows = jnp.dot(pick_v[...], slabs(hi, slots[zl]), preferred_element_type=F32).astype(BF16)
                for p in range(4):
                    W[hi, p, zl * 64 : zl * 64 + 64] = sorted_rows[p * 64 : p * 64 + 64]
            kv = half_silu(0.5 * nt_dot(H[...].reshape(512, 1024), W[hi, 0:2].reshape(256, 1024)))
            KV[t, hi, c, :, :128] = kv[:, :128].astype(BF16)
            KV[t, hi, c, :, 128:] = (kv[:, 128:] * mask_v[...]).astype(BF16)
            kv_copy(t, hi, c).start()
            return carry

        lax.fori_loop(0, 2, keys_values, 0)

        def attend(hi, carry):
            for w in (3, 4):
                @pl.when((t == w - 3) & (hi == 0))
                def _():
                    third_second(w)

            for w in (2, 3, 4):
                @pl.when((t == w - 2) & (hi == 1))
                def _():
                    ring_wait(w)
                    if w < 4:
                        ring_send(w + 1)
                    settle(stage3[w][0][2] + stage3[w][1][2])
                    twin_send(w)

            kv_copy(t, hi, oc).wait_recv()
            h = hi * 4 + pair
            at = pl.ds(pl.multiple_of(h * 128, 128), 128)
            for user in range(users_here):
                rows_c = cand_v[user]
                qg = half_silu(0.5 * nt_dot(rows_c, W[hi, 2:4].reshape(256, 1024))).astype(BF16)
                kv_c = half_silu(0.5 * nt_dot(rows_c, W[hi, 0:2].reshape(256, 1024))).astype(BF16)
                queries = qg[:, :128]
                gate[user, :, at] = qg[:, 128:]
                keys, values = KV[t, hi, user, :, :128], KV[t, hi, user, :, 128:]
                weights = half_silu(nt_dot(queries, keys) * score_half).astype(BF16)
                att = jnp.dot(weights, values, preferred_element_type=F32)
                own = jnp.sum(queries.astype(F32) * kv_c[:, :128].astype(F32), axis=1, keepdims=True)
                own = half_silu(own * score_half)
                attn[user, :, at] = att + own * kv_c[:, 128:].astype(F32)
            return carry

        lax.fori_loop(0, 2, attend, 0)
        return carry

    def kv_copy(t, hi, whose):
        k = kv_sems[0] + t * 2 + hi
        return pltpu.make_async_remote_copy(
            src_ref=KV.at[t, hi, whose], dst_ref=KV.at[t, hi, whose],
            send_sem=send_sem.at[k], recv_sem=recv_sem.at[k], device_id=sib, device_id_type=MESH,
        )

    lax.fori_loop(0, HEADS // 2, chunk, 0)

    slot0 = s * 384

    def norm(user, block):
        rows_a = attn[user, block]
        mean = jnp.sum(rows_a, axis=1, keepdims=True) * (1.0 / 1024)
        centered = rows_a - mean
        var = jnp.sum(centered * centered, axis=1, keepdims=True) * (1.0 / 1024)
        normed = centered * lax.rsqrt(var + 1e-06)
        gated[user, block] = (normed * gate[user, block].astype(F32)).astype(BF16)

    def norm_step(i, carry):
        norm(0, pl.ds(pl.multiple_of(i * 64, 64), 64))
        return carry

    lax.fori_loop(0, 6, norm_step, 0)
    for user in range(users_here):
        for n in range(4):
            ncols = pl.ds(n * 256, 256)
            mixed = jnp.dot(gated[user], ow_v[:, ncols], preferred_element_type=F32)
            mixed = mixed + cand_v[user, :, ncols].astype(F32)
            slot = slot0 + lax.broadcasted_iota(jnp.int32, (384, 256), 0)
            out_v[user, :, ncols] = jnp.where(slot < ccount_ref[user], mixed, 0.0).astype(BF16)
            if user == 0:
                for piece in range(3):
                    norm(1, pl.ds(n * 96 + piece * 32, 32))
        pltpu.make_async_copy(out_v.at[user], out_ref.at[user], local_sem.at[3 + user]).start()
    for user in range(users_here):
        pltpu.make_async_copy(out_v.at[user], out_ref.at[user], local_sem.at[3 + user]).wait()
    for number in range(HEADS):
        kv_copy(number // 2, number % 2, c).wait_send()
    for src, k in sent:
        rcopy(src, src, k, sib).wait_send()
    assert state["k"] <= NSEM


def body(candidates, history, proj_weight, out_weight, hist_len, cand_count):
    anyspace = pl.BlockSpec(memory_space=pl.ANY)
    smem = pl.BlockSpec(memory_space=pltpu.SMEM)
    vmem = pl.BlockSpec(memory_space=pltpu.VMEM)
    return pl.pallas_call(
        kernel,
        out_shape=jax.ShapeDtypeStruct(candidates.shape, BF16),
        in_specs=[anyspace, anyspace, vmem, anyspace, smem, smem],
        out_specs=anyspace,
        scratch_shapes=[
            pltpu.VMEM((2, NX, NY, NZ, 16, 1024), BF16),
            pltpu.VMEM((NX, 2, 2, 32, 1024), BF16),
            pltpu.VMEM((4, 2, 2, 512, 256), BF16),
            pltpu.VMEM((2, 4, 128, 1024), BF16),
            pltpu.VMEM((256, 256), BF16),
            pltpu.VMEM((2, 384, 1024), BF16),
            pltpu.VMEM((1024, 1024), BF16),
            pltpu.VMEM((512, 128), F32),
            pltpu.VMEM((2, 384, 1024), F32),
            pltpu.VMEM((2, 384, 1024), BF16),
            pltpu.VMEM((2, 384, 1024), BF16),
            pltpu.VMEM((2, 384, 1024), BF16),
            pltpu.SemaphoreType.DMA((NSEM,)),
            pltpu.SemaphoreType.DMA((NSEM,)),
            pltpu.SemaphoreType.DMA((5,)),
        ],
        compiler_params=pltpu.CompilerParams(
            collective_id=0, has_side_effects=True, vmem_limit_bytes=56 * 1024 * 1024
        ),
    )(candidates, history, proj_weight, out_weight, hist_len, cand_count)


def solution(mesh):
    in_specs = (
        P("users", "score", None),
        P("users", "score", None),
        P(("users", "score"), None, None),
        P(),
        P("users"),
        P("users"),
    )
    out_specs = P("users", "score", None)
    return jax.shard_map(body, mesh=mesh, in_specs=in_specs, out_specs=out_specs, check_vma=False)
```

```python
import functools
import math

import jax
import jax.numpy as jnp
from jax import lax
from jax.experimental import pallas as pl
from jax.experimental.pallas import tpu as pltpu
from jax.sharding import PartitionSpec as P

MESH = pl.DeviceIdType.MESH
HEADS = 8
NX, NY, NZ = 4, 4, 8
BF16, F32 = jnp.bfloat16, jnp.float32
COLS_X, COLS_Y, COLS_Z = pl.ds(0, 256), pl.ds(256, 384), pl.ds(640, 384)
COLS_XY = pl.ds(0, 640)
SLOT = {0: 0, -1: 1, 1: 2, -2: 3, 2: 4, -3: 5, 3: 6, 4: 7, -4: 7}
NSEM = 128


def nt_dot(a, b):
    return lax.dot_general(a, b, (((1,), (1,)), ((), ())), preferred_element_type=F32)


def half_silu(t):
    return t + t * jnp.tanh(t)


def kernel(
    cand_ref, hist_ref, proj_ref, ow_ref, hlen_ref, ccount_ref, out_ref,
    G, H, KV, W, pick_v, cand_v, ow_v, mask_v, attn, gate, gated, out_v, send_sem, recv_sem, local_sem,
):
    u = lax.axis_index("users")
    s = lax.axis_index("score")
    z = lax.rem(u, NZ)
    yhi = lax.div(u, NZ)
    c = lax.rem(s, 2)
    x = lax.rem(lax.div(s, 2), NX)
    ylo = lax.div(s, 8)
    y = yhi * 2 + ylo
    oc = 1 - c

    def dev(px, py, pz, pc):
        return (lax.div(py, 2) * NZ + pz, lax.rem(py, 2) * 8 + px * 2 + pc)

    def up(pos, n, k):
        return lax.rem(pos + k + n, n)

    yo = y + 1 - 2 * ylo
    sib = dev(x, y, z, oc)
    local = [
        pltpu.make_async_copy(hist_ref.at[c], H.at[x, ylo, c], local_sem.at[0]),
        pltpu.make_async_copy(cand_ref, cand_v, local_sem.at[1]),
        pltpu.make_async_copy(ow_ref, ow_v, local_sem.at[2]),
    ]
    for copy in local:
        copy.start()

    barrier = pltpu.get_barrier_semaphore()
    partners = [dev(up(x, NX, k), y, z, c) for k in (1, 3, 2)] + [dev(x, up(y, NY, k), z, c) for k in (1, 3, 2)]
    partners += [dev(x, y, up(z, NZ, k), c) for k in (1, 7, 2, 6, 3, 5, 4)] + [sib, dev(x, yo, z, oc)]
    for partner in partners:
        pl.semaphore_signal(barrier, inc=1, device_id=partner, device_id_type=MESH)

    row16 = lax.broadcasted_iota(jnp.int32, (16, 1024), 0)
    tile = jnp.zeros((16, 1024), F32)
    for f in range(4):
        rows_f = proj_ref[f].astype(F32)
        for p in range(4):
            tile = jnp.where(row16 == f * 4 + p, jnp.broadcast_to(rows_f[p : p + 1], (16, 1024)), tile)
    G[c, x, y, 0] = tile.astype(BF16)

    pl.semaphore_wait(barrier, len(partners))

    state = {"k": 0}
    sent = []

    def new_sem():
        k = state["k"]
        state["k"] = k + 1
        return k

    def rcopy(src, dst, k, target):
        return pltpu.make_async_remote_copy(
            src_ref=src(), dst_ref=dst(), send_sem=send_sem.at[k], recv_sem=recv_sem.at[k],
            device_id=target, device_id_type=MESH,
        )

    def send(src, dst, k, target):
        rcopy(src, dst, k, target).start()
        sent.append((src, k))

    def wait(dst, k):
        rcopy(dst, dst, k, sib).wait_recv()

    hist_arrivals = []
    for who, target, py, pc in (
        (oc, sib, ylo, oc), (c, dev(x, yo, z, c), 1 - ylo, c), (oc, dev(x, yo, z, oc), 1 - ylo, oc),
    ):
        k = new_sem()
        send(functools.partial(hist_ref.at.__getitem__, who), lambda: H.at[x, ylo, c], k, target)
        hist_arrivals.append((functools.partial(H.at.__getitem__, (x, py, pc)), k))

    whole = slice(None)

    def view(plane, xs, ys, slots, columns):
        return lambda: G.at[plane, xs, ys, slots, :, columns]

    def direct(axis, block):
        n, at = (NX, x) if axis == "x" else (NY, y)
        arrivals = []
        for step in (1, 3, 2):
            k = new_sem()
            to = up(at, n, step)
            send(block(at), block(at), k, dev(to, y, z, c) if axis == "x" else dev(x, to, z, c))
            arrivals.append((block(up(at, n, -step)), k))
        return arrivals

    def settle(arrivals):
        for where, k in arrivals:
            wait(where, k)

    waves = [pl.ds(0, 1), pl.ds(1, 2), pl.ds(3, 2), pl.ds(5, 2), pl.ds(7, 1)]

    def second(w):
        group_x = direct("y", lambda at: view(c, x, at, waves[w], COLS_X))
        group_y = direct("x", lambda at: view(c, at, y, waves[w], COLS_Y))
        return group_x, group_y

    def third(w, arrivals):
        settle(arrivals[0])
        group_x = direct("x", lambda at: view(c, at, whole, waves[w], COLS_X))
        settle(arrivals[1])
        group_y = direct("y", lambda at: view(c, whole, at, waves[w], COLS_Y))
        return group_x + group_y

    spot = {"x": [up(x, NX, k) for k in range(NX)], "y": [up(y, NY, k) for k in range(NY)]}
    neighbour = {
        "x": [dev(spot["x"][k], y, z, c) for k in range(NX)],
        "y": [dev(x, spot["y"][k], z, c) for k in range(NY)],
    }

    def ring_plan(axis, block):
        first = [(block(spot[axis][3], None), new_sem()), (block(spot[axis][1], None), new_sem())]
        return first, [(block(spot[axis][2], half), new_sem()) for half in range(2)]

    def ring_first(axis, block, plan):
        for (_, k), step in zip(plan[0], (1, 3)):
            send(block(spot[axis][0], None), block(spot[axis][0], None), k, neighbour[axis][step])

    def ring_second(axis, block, plan):
        settle(plan[0])
        for half, step in ((0, 1), (1, 3)):
            mine = block(spot[axis][4 - step], half)
            send(mine, mine, plan[1][half][1], neighbour[axis][step])

    def part(half):
        return whole if half is None else pl.ds(2 * half, 2)

    def wave_x(w):
        return "x", lambda at, half: view(c, at, part(half), waves[w], COLS_X)

    def wave_y(w):
        return "y", lambda at, half: view(c, part(half), at, waves[w], COLS_Y)

    plans = {w: (ring_plan(*wave_x(w)), ring_plan(*wave_y(w))) for w in (2, 3, 4)}

    def third_first(w):
        settle(stage2[w][0])
        ring_first(*wave_x(w), plans[w][0])
        settle(stage2[w][1])
        ring_first(*wave_y(w), plans[w][1])

    def third_second(w):
        ring_second(*wave_x(w), plans[w][0])
        ring_second(*wave_y(w), plans[w][1])

    def hist_block(at, half):
        return (lambda: H.at[at]) if half is None else (lambda: H.at[at, half])

    hist_plan = ring_plan("x", hist_block)
    along_z = {}

    def z_send(off):
        k = new_sem()
        send(view(c, x, y, 0, COLS_XY), view(c, x, y, SLOT[-off], COLS_XY), k, dev(x, y, up(z, NZ, off), c))
        along_z[SLOT[-off]] = (view(c, x, y, SLOT[-off], COLS_XY), k)

    zx = direct("x", lambda at: view(c, at, y, 0, COLS_Z))
    z_send(1)
    z_send(-1)
    stage2 = {0: second(0)}
    for off in (2, -2, 3, -3, 4):
        z_send(off)
    local[0].wait()
    settle(hist_arrivals)
    ring_first("x", hist_block, hist_plan)
    settle(zx)
    zy = direct("y", lambda at: view(c, whole, at, 0, COLS_Z))
    stage3 = {0: third(0, stage2[0])}
    settle([along_z[1], along_z[2]])
    stage2[1] = second(1)
    settle(zy)

    z_right, z_left = dev(x, y, up(z, NZ, 1), c), dev(x, y, up(z, NZ, -1), c)
    ring_sems = [(new_sem(), new_sem()) for _ in range(4)]
    twin_sems = [new_sem() for _ in range(5)]
    kv_sems = [new_sem() for _ in range(HEADS)]

    def ring_blocks(w):
        xs = (whole, whole) if w < 4 else (pl.ds(0, 2), pl.ds(2, 2))
        down, high = (2 * w - 3, 2 * w - 2) if w > 1 else (0, 0)
        into = (2 * w - 1, 2 * w) if w < 4 else (7, 7)
        return [
            (view(c, xs[0], whole, down, COLS_Z), view(c, xs[0], whole, into[0], COLS_Z)),
            (view(c, xs[1], whole, high, COLS_Z), view(c, xs[1], whole, into[1], COLS_Z)),
        ]

    def ring_send(w):
        for (src, dst), k, target in zip(ring_blocks(w), ring_sems[w - 1], (z_right, z_left)):
            send(src, dst, k, target)

    def ring_wait(w):
        for (_, dst), k in zip(ring_blocks(w), ring_sems[w - 1]):
            wait(dst, k)

    def twin_send(w):
        block = view(c, whole, whole, waves[w], whole)
        send(block, block, twin_sems[w], sib)

    def twin_wait(w):
        wait(view(oc, whole, whole, waves[w], whole), twin_sems[w])

    ring_send(1)
    stage3[1] = third(1, stage2[1])
    settle([along_z[3], along_z[4]])
    stage2[2] = second(2)
    ring_second("x", hist_block, hist_plan)
    settle(stage3[0])
    twin_send(0)
    third_first(2)
    ring_wait(1)
    ring_send(2)
    settle(stage3[1])
    twin_send(1)
    settle([along_z[5], along_z[6], along_z[7]])
    stage2[3] = second(3)
    stage2[4] = second(4)
    third_second(2)
    local[1].wait()
    local[2].wait()
    settle(hist_plan[1])
    twin_wait(0)
    twin_wait(1)

    head_size = 128
    score_half = 0.5 / math.sqrt(head_size)
    users_here = cand_v.shape[0]

    q = lax.broadcasted_iota(jnp.int32, (512, 128), 0)
    event = (((q >> 6) & 1) * 8 + (q >> 7) * 2 + ((q >> 5) & 1)) * 32 + (q & 31)
    mask_v[...] = (event < hlen_ref[c]).astype(F32)
    out_row = lax.broadcasted_iota(jnp.int32, (256, 256), 0)
    in_row = lax.broadcasted_iota(jnp.int32, (256, 256), 1)
    source = ((out_row & 63) >> 2) * 16 + (out_row & 3) * 4 + (out_row >> 6)
    pick_v[...] = (in_row == source).astype(F32).astype(BF16)

    odd = lax.rem(z, 2)

    def slabs(hi, slot):
        return jnp.concatenate(
            [G[plane, px, hi * 2 + yl, slot] for yl in range(2) for px in range(NX) for plane in range(2)],
            axis=0,
        )

    def choose(t, even_slots, odd_slots):
        slot = jnp.int32(0)
        for number in range(4):
            slot = jnp.where(t == number, jnp.where(odd == 1, odd_slots[number], even_slots[number]), slot)
        return slot

    def chunk(t, carry):
        for w in (2, 3, 4):
            @pl.when(t == w - 1)
            def _():
                twin_wait(w)

        turn = t + lax.div(t, 2) - 2 * lax.div(t, 3)
        pair = lax.rem(lax.div(z, 2) + (2 * odd - 1) * turn + 8, 4)
        slots = (choose(t, (0, 3, 4, 7), (1, 2, 5, 6)), choose(t, (2, 1, 6, 5), (0, 4, 3, 7)))

        def keys_values(hi, carry):
            for zl in range(2):
                sorted_rows = jnp.dot(pick_v[...], slabs(hi, slots[zl]), preferred_element_type=F32).astype(BF16)
                for p in range(4):
                    W[hi, p, zl * 64 : zl * 64 + 64] = sorted_rows[p * 64 : p * 64 + 64]
            kv = half_silu(0.5 * nt_dot(H[...].reshape(512, 1024), W[hi, 0:2].reshape(256, 1024)))
            KV[t, hi, c, :, :128] = kv[:, :128].astype(BF16)
            KV[t, hi, c, :, 128:] = (kv[:, 128:] * mask_v[...]).astype(BF16)
            kv_copy(t, hi, c).start()
            return carry

        lax.fori_loop(0, 2, keys_values, 0)

        def attend(hi, carry):
            @pl.when((t == 0) & (hi == 0))
            def _():
                third_first(3)
                third_first(4)

            @pl.when((t == 0) & (hi == 1))
            def _():
                third_second(3)
                third_second(4)

            for w in (2, 3, 4):
                @pl.when((t == w - 2) & (hi == 0))
                def _():
                    ring_wait(w)
                    if w < 4:
                        ring_send(w + 1)
                    settle(plans[w][0][1] + plans[w][1][1])
                    twin_send(w)

            h = hi * 4 + pair
            at = pl.ds(pl.multiple_of(h * 128, 128), 128)
            for user in (c, oc):
                if user is oc:
                    kv_copy(t, hi, oc).wait_recv()
                rows_c = cand_v[user]
                qg = half_silu(0.5 * nt_dot(rows_c, W[hi, 2:4].reshape(256, 1024))).astype(BF16)
                kv_c = half_silu(0.5 * nt_dot(rows_c, W[hi, 0:2].reshape(256, 1024))).astype(BF16)
                queries = qg[:, :128]
                gate[user, :, at] = qg[:, 128:]
                keys, values = KV[t, hi, user, :, :128], KV[t, hi, user, :, 128:]
                weights = half_silu(nt_dot(queries, keys) * score_half).astype(BF16)
                att = jnp.dot(weights, values, preferred_element_type=F32)
                own = jnp.sum(queries.astype(F32) * kv_c[:, :128].astype(F32), axis=1, keepdims=True)
                own = half_silu(own * score_half)
                attn[user, :, at] = att + own * kv_c[:, 128:].astype(F32)
            return carry

        lax.fori_loop(0, 2, attend, 0)
        return carry

    def kv_copy(t, hi, whose):
        k = kv_sems[0] + t * 2 + hi
        return pltpu.make_async_remote_copy(
            src_ref=KV.at[t, hi, whose], dst_ref=KV.at[t, hi, whose],
            send_sem=send_sem.at[k], recv_sem=recv_sem.at[k], device_id=sib, device_id_type=MESH,
        )

    lax.fori_loop(0, HEADS // 2, chunk, 0)

    slot0 = s * 384

    def norm(user, block):
        rows_a = attn[user, block]
        mean = jnp.sum(rows_a, axis=1, keepdims=True) * (1.0 / 1024)
        centered = rows_a - mean
        var = jnp.sum(centered * centered, axis=1, keepdims=True) * (1.0 / 1024)
        normed = centered * lax.rsqrt(var + 1e-06)
        gated[user, block] = (normed * gate[user, block].astype(F32)).astype(BF16)

    def norm_step(i, carry):
        norm(0, pl.ds(pl.multiple_of(i * 64, 64), 64))
        return carry

    lax.fori_loop(0, 6, norm_step, 0)
    for user in range(users_here):
        for n in range(4):
            ncols = pl.ds(n * 256, 256)
            mixed = jnp.dot(gated[user], ow_v[:, ncols], preferred_element_type=F32)
            mixed = mixed + cand_v[user, :, ncols].astype(F32)
            slot = slot0 + lax.broadcasted_iota(jnp.int32, (384, 256), 0)
            out_v[user, :, ncols] = jnp.where(slot < ccount_ref[user], mixed, 0.0).astype(BF16)
            if user == 0:
                for piece in range(3):
                    norm(1, pl.ds(n * 96 + piece * 32, 32))
        pltpu.make_async_copy(out_v.at[user], out_ref.at[user], local_sem.at[3 + user]).start()
    for user in range(users_here):
        pltpu.make_async_copy(out_v.at[user], out_ref.at[user], local_sem.at[3 + user]).wait()
    for number in range(HEADS):
        kv_copy(number // 2, number % 2, c).wait_send()
    for src, k in sent:
        rcopy(src, src, k, sib).wait_send()
    assert state["k"] <= NSEM


def body(candidates, history, proj_weight, out_weight, hist_len, cand_count):
    anyspace = pl.BlockSpec(memory_space=pl.ANY)
    smem = pl.BlockSpec(memory_space=pltpu.SMEM)
    vmem = pl.BlockSpec(memory_space=pltpu.VMEM)
    return pl.pallas_call(
        kernel,
        out_shape=jax.ShapeDtypeStruct(candidates.shape, BF16),
        in_specs=[anyspace, anyspace, vmem, anyspace, smem, smem],
        out_specs=anyspace,
        scratch_shapes=[
            pltpu.VMEM((2, NX, NY, NZ, 16, 1024), BF16),
            pltpu.VMEM((NX, 2, 2, 32, 1024), BF16),
            pltpu.VMEM((4, 2, 2, 512, 256), BF16),
            pltpu.VMEM((2, 4, 128, 1024), BF16),
            pltpu.VMEM((256, 256), BF16),
            pltpu.VMEM((2, 384, 1024), BF16),
            pltpu.VMEM((1024, 1024), BF16),
            pltpu.VMEM((512, 128), F32),
            pltpu.VMEM((2, 384, 1024), F32),
            pltpu.VMEM((2, 384, 1024), BF16),
            pltpu.VMEM((2, 384, 1024), BF16),
            pltpu.VMEM((2, 384, 1024), BF16),
            pltpu.SemaphoreType.DMA((NSEM,)),
            pltpu.SemaphoreType.DMA((NSEM,)),
            pltpu.SemaphoreType.DMA((5,)),
        ],
        compiler_params=pltpu.CompilerParams(
            collective_id=0, has_side_effects=True, vmem_limit_bytes=56 * 1024 * 1024
        ),
    )(candidates, history, proj_weight, out_weight, hist_len, cand_count)


def solution(mesh):
    in_specs = (
        P("users", "score", None),
        P("users", "score", None),
        P(("users", "score"), None, None),
        P(),
        P("users"),
        P("users"),
    )
    out_specs = P("users", "score", None)
    return jax.shard_map(body, mesh=mesh, in_specs=in_specs, out_specs=out_specs, check_vma=False)
```

```python
import functools
import math

import jax
import jax.numpy as jnp
from jax import lax
from jax.experimental import pallas as pl
from jax.experimental.pallas import tpu as pltpu
from jax.sharding import PartitionSpec as P

MESH = pl.DeviceIdType.MESH
HEADS = 8
NX, NY, NZ = 4, 4, 8
BF16, F32 = jnp.bfloat16, jnp.float32
COLS_X, COLS_Y, COLS_Z = pl.ds(0, 256), pl.ds(256, 384), pl.ds(640, 384)
COLS_XY = pl.ds(0, 640)
SLOT = {0: 0, -1: 1, 1: 2, -2: 3, 2: 4, -3: 5, 3: 6, 4: 7, -4: 7}
NSEM = 128


def nt_dot(a, b):
    return lax.dot_general(a, b, (((1,), (1,)), ((), ())), preferred_element_type=F32)


def half_silu(t):
    return t + t * jnp.tanh(t)


def kernel(
    cand_ref, hist_ref, proj_ref, ow_ref, hlen_ref, ccount_ref, out_ref,
    G, H, KV, Q, W, pick_v, cand_v, ow_v, mask_v, attn, gate, gated, out_v, send_sem, recv_sem, local_sem,
):
    u = lax.axis_index("users")
    s = lax.axis_index("score")
    z = lax.rem(u, NZ)
    yhi = lax.div(u, NZ)
    c = lax.rem(s, 2)
    x = lax.rem(lax.div(s, 2), NX)
    ylo = lax.div(s, 8)
    y = yhi * 2 + ylo
    oc = 1 - c

    def dev(px, py, pz, pc):
        return (lax.div(py, 2) * NZ + pz, lax.rem(py, 2) * 8 + px * 2 + pc)

    def up(pos, n, k):
        return lax.rem(pos + k + n, n)

    yo = y + 1 - 2 * ylo
    sib = dev(x, y, z, oc)
    local = [
        pltpu.make_async_copy(hist_ref.at[c], H.at[x, ylo, c], local_sem.at[0]),
        pltpu.make_async_copy(cand_ref, cand_v, local_sem.at[1]),
        pltpu.make_async_copy(ow_ref, ow_v, local_sem.at[2]),
    ]
    for copy in local:
        copy.start()

    barrier = pltpu.get_barrier_semaphore()
    partners = [dev(up(x, NX, k), y, z, c) for k in (1, 3, 2)] + [dev(x, up(y, NY, k), z, c) for k in (1, 3, 2)]
    partners += [dev(x, y, up(z, NZ, k), c) for k in (1, 7, 2, 6, 3, 5, 4)] + [sib, dev(x, yo, z, oc)]
    for partner in partners:
        pl.semaphore_signal(barrier, inc=1, device_id=partner, device_id_type=MESH)

    row16 = lax.broadcasted_iota(jnp.int32, (16, 1024), 0)
    tile = jnp.zeros((16, 1024), F32)
    for f in range(4):
        rows_f = proj_ref[f].astype(F32)
        for p in range(4):
            tile = jnp.where(row16 == f * 4 + p, jnp.broadcast_to(rows_f[p : p + 1], (16, 1024)), tile)
    G[c, x, y, 0] = tile.astype(BF16)

    pl.semaphore_wait(barrier, len(partners))

    state = {"k": 0}
    sent = []

    def new_sem():
        k = state["k"]
        state["k"] = k + 1
        return k

    def rcopy(src, dst, k, target):
        return pltpu.make_async_remote_copy(
            src_ref=src(), dst_ref=dst(), send_sem=send_sem.at[k], recv_sem=recv_sem.at[k],
            device_id=target, device_id_type=MESH,
        )

    def send(src, dst, k, target):
        rcopy(src, dst, k, target).start()
        sent.append((src, k))

    def wait(dst, k):
        rcopy(dst, dst, k, sib).wait_recv()

    hist_arrivals = []
    for who, target, py, pc in (
        (oc, sib, ylo, oc), (c, dev(x, yo, z, c), 1 - ylo, c), (oc, dev(x, yo, z, oc), 1 - ylo, oc),
    ):
        k = new_sem()
        send(functools.partial(hist_ref.at.__getitem__, who), lambda: H.at[x, ylo, c], k, target)
        hist_arrivals.append((functools.partial(H.at.__getitem__, (x, py, pc)), k))

    whole = slice(None)

    def view(plane, xs, ys, slots, columns):
        return lambda: G.at[plane, xs, ys, slots, :, columns]

    def direct(axis, block):
        n, at = (NX, x) if axis == "x" else (NY, y)
        arrivals = []
        for step in (1, 3, 2):
            k = new_sem()
            to = up(at, n, step)
            send(block(at), block(at), k, dev(to, y, z, c) if axis == "x" else dev(x, to, z, c))
            arrivals.append((block(up(at, n, -step)), k))
        return arrivals

    def settle(arrivals):
        for where, k in arrivals:
            wait(where, k)

    waves = [pl.ds(0, 1), pl.ds(1, 2), pl.ds(3, 2), pl.ds(5, 2), pl.ds(7, 1)]

    def second(w):
        group_x = direct("y", lambda at: view(c, x, at, waves[w], COLS_X))
        group_y = direct("x", lambda at: view(c, at, y, waves[w], COLS_Y))
        return group_x, group_y

    def third(w, arrivals):
        settle(arrivals[0])
        group_x = direct("x", lambda at: view(c, at, whole, waves[w], COLS_X))
        settle(arrivals[1])
        group_y = direct("y", lambda at: view(c, whole, at, waves[w], COLS_Y))
        return group_x + group_y

    spot = {"x": [up(x, NX, k) for k in range(NX)], "y": [up(y, NY, k) for k in range(NY)]}
    neighbour = {
        "x": [dev(spot["x"][k], y, z, c) for k in range(NX)],
        "y": [dev(x, spot["y"][k], z, c) for k in range(NY)],
    }

    def ring_plan(axis, block):
        first = [(block(spot[axis][3], None), new_sem()), (block(spot[axis][1], None), new_sem())]
        return first, [(block(spot[axis][2], half), new_sem()) for half in range(2)]

    def ring_first(axis, block, plan):
        for (_, k), step in zip(plan[0], (1, 3)):
            send(block(spot[axis][0], None), block(spot[axis][0], None), k, neighbour[axis][step])

    def ring_second(axis, block, plan):
        settle(plan[0])
        for half, step in ((0, 1), (1, 3)):
            mine = block(spot[axis][4 - step], half)
            send(mine, mine, plan[1][half][1], neighbour[axis][step])

    def part(half):
        return whole if half is None else pl.ds(2 * half, 2)

    def wave_x(w):
        return "x", lambda at, half: view(c, at, part(half), waves[w], COLS_X)

    def wave_y(w):
        return "y", lambda at, half: view(c, part(half), at, waves[w], COLS_Y)

    plans = {w: (ring_plan(*wave_x(w)), ring_plan(*wave_y(w))) for w in (2, 3, 4)}

    def third_first(w):
        settle(stage2[w][0])
        ring_first(*wave_x(w), plans[w][0])
        settle(stage2[w][1])
        ring_first(*wave_y(w), plans[w][1])

    def third_second(w):
        ring_second(*wave_x(w), plans[w][0])
        ring_second(*wave_y(w), plans[w][1])

    def hist_block(at, half):
        return (lambda: H.at[at]) if half is None else (lambda: H.at[at, half])

    hist_plan = ring_plan("x", hist_block)
    along_z = {}

    def z_send(off):
        k = new_sem()
        send(view(c, x, y, 0, COLS_XY), view(c, x, y, SLOT[-off], COLS_XY), k, dev(x, y, up(z, NZ, off), c))
        along_z[SLOT[-off]] = (view(c, x, y, SLOT[-off], COLS_XY), k)

    zx = direct("x", lambda at: view(c, at, y, 0, COLS_Z))
    z_send(1)
    z_send(-1)
    stage2 = {0: second(0)}
    for off in (2, -2, 3, -3, 4):
        z_send(off)
    settle(zx)
    zy = direct("y", lambda at: view(c, whole, at, 0, COLS_Z))
    stage3 = {0: third(0, stage2[0])}
    settle([along_z[1], along_z[2]])
    stage2[1] = second(1)
    settle(zy)

    z_right, z_left = dev(x, y, up(z, NZ, 1), c), dev(x, y, up(z, NZ, -1), c)
    ring_sems = [(new_sem(), new_sem()) for _ in range(4)]
    twin_sems = [new_sem() for _ in range(5)]
    kv_sems = [new_sem() for _ in range(HEADS)]

    def ring_blocks(w):
        xs = (whole, whole) if w < 4 else (pl.ds(0, 2), pl.ds(2, 2))
        down, high = (2 * w - 3, 2 * w - 2) if w > 1 else (0, 0)
        into = (2 * w - 1, 2 * w) if w < 4 else (7, 7)
        return [
            (view(c, xs[0], whole, down, COLS_Z), view(c, xs[0], whole, into[0], COLS_Z)),
            (view(c, xs[1], whole, high, COLS_Z), view(c, xs[1], whole, into[1], COLS_Z)),
        ]

    def ring_send(w):
        for (src, dst), k, target in zip(ring_blocks(w), ring_sems[w - 1], (z_right, z_left)):
            send(src, dst, k, target)

    def ring_wait(w):
        for (_, dst), k in zip(ring_blocks(w), ring_sems[w - 1]):
            wait(dst, k)

    def twin_send(w):
        block = view(c, whole, whole, waves[w], whole)
        send(block, block, twin_sems[w], sib)

    def twin_wait(w):
        wait(view(oc, whole, whole, waves[w], whole), twin_sems[w])

    ring_send(1)
    stage3[1] = third(1, stage2[1])
    local[0].wait()
    settle(hist_arrivals)
    ring_first("x", hist_block, hist_plan)
    settle([along_z[3], along_z[4]])
    stage2[2] = second(2)
    settle(stage3[0])
    twin_send(0)
    settle([along_z[5], along_z[6], along_z[7]])
    stage2[3] = second(3)
    stage2[4] = second(4)
    ring_wait(1)
    ring_send(2)
    settle(stage3[1])
    twin_send(1)
    third_first(2)
    ring_second("x", hist_block, hist_plan)
    local[1].wait()
    local[2].wait()
    twin_wait(0)
    twin_wait(1)

    head_size = 128
    score_half = 0.5 / math.sqrt(head_size)
    users_here = cand_v.shape[0]

    q = lax.broadcasted_iota(jnp.int32, (512, 128), 0)
    event = (((q >> 6) & 1) * 8 + (q >> 7) * 2 + ((q >> 5) & 1)) * 32 + (q & 31)
    mask_v[...] = (event < hlen_ref[c]).astype(F32)
    out_row = lax.broadcasted_iota(jnp.int32, (256, 256), 0)
    in_row = lax.broadcasted_iota(jnp.int32, (256, 256), 1)
    source = ((out_row & 63) >> 2) * 16 + (out_row & 3) * 4 + (out_row >> 6)
    pick_v[...] = (in_row == source).astype(F32).astype(BF16)

    odd = lax.rem(z, 2)

    def slabs(hi, slot):
        return jnp.concatenate(
            [G[plane, px, hi * 2 + yl, slot] for yl in range(2) for px in range(NX) for plane in range(2)],
            axis=0,
        )

    def choose(t, even_slots, odd_slots):
        slot = jnp.int32(0)
        for number in range(4):
            slot = jnp.where(t == number, jnp.where(odd == 1, odd_slots[number], even_slots[number]), slot)
        return slot

    def pair_of(t):
        turn = t + lax.div(t, 2) - 2 * lax.div(t, 3)
        return lax.rem(lax.div(z, 2) + (2 * odd - 1) * turn + 8, 4)

    def columns_of(t, hi):
        return pl.ds(pl.multiple_of((hi * 4 + pair_of(t)) * 128, 128), 128)

    def project(t, hi):
        slots = (choose(t, (0, 3, 4, 7), (1, 2, 5, 6)), choose(t, (2, 1, 6, 5), (0, 4, 3, 7)))
        keep, at = lax.rem(t, 2), columns_of(t, hi)
        for zl in range(2):
            sorted_rows = jnp.dot(pick_v[...], slabs(hi, slots[zl]), preferred_element_type=F32).astype(BF16)
            for p in range(4):
                W[keep, hi, p, zl * 64 : zl * 64 + 64] = sorted_rows[p * 64 : p * 64 + 64]
        for user in range(users_here):
            rows_c = cand_v[user]
            qg = half_silu(0.5 * nt_dot(rows_c, W[keep, hi, 2:4].reshape(256, 1024))).astype(BF16)
            kv_c = half_silu(0.5 * nt_dot(rows_c, W[keep, hi, 0:2].reshape(256, 1024))).astype(BF16)
            queries = qg[:, :128]
            Q[keep, hi, user] = queries
            gate[user, :, at] = qg[:, 128:]
            own = jnp.sum(queries.astype(F32) * kv_c[:, :128].astype(F32), axis=1, keepdims=True)
            attn[user, :, at] = half_silu(own * score_half) * kv_c[:, 128:].astype(F32)

    def keys_values(t, hi):
        w_kv = W[lax.rem(t, 2), hi, 0:2].reshape(256, 1024)
        kv = half_silu(0.5 * nt_dot(H[...].reshape(512, 1024), w_kv))
        KV[t, hi, c, :, :128] = kv[:, :128].astype(BF16)
        KV[t, hi, c, :, 128:] = (kv[:, 128:] * mask_v[...]).astype(BF16)
        kv_copy(t, hi, c).start()

    def attend(t, hi):
        kv_copy(t, hi, oc).wait_recv()
        keep, at = lax.rem(t, 2), columns_of(t, hi)
        for user in range(users_here):
            keys, values = KV[t, hi, user, :, :128], KV[t, hi, user, :, 128:]
            weights = half_silu(nt_dot(Q[keep, hi, user], keys) * score_half).astype(BF16)
            attn[user, :, at] += jnp.dot(weights, values, preferred_element_type=F32)

    def both(work, t):
        def step(hi, carry):
            work(t, hi)
            return carry

        lax.fori_loop(0, 2, step, 0)

    def chunk(t, carry):
        @pl.when(t == 1)
        def _():
            settle(hist_plan[1])

        @pl.when(t > 0)
        def _():
            both(keys_values, t - 1)

        for w in (2, 3, 4):
            @pl.when(t == w - 1)
            def _():
                twin_wait(w)

        @pl.when(t < 4)
        def _():
            both(project, t)

        @pl.when(t == 0)
        def _():
            third_second(2)
            third_first(3)
            third_first(4)

        for w in (2, 3, 4):
            @pl.when(t == w - 2)
            def _():
                ring_wait(w)
                if w < 4:
                    ring_send(w + 1)
                if w == 2:
                    third_second(3)
                if w == 3:
                    third_second(4)
                settle(plans[w][0][1] + plans[w][1][1])
                twin_send(w)

        @pl.when(t > 0)
        def _():
            both(attend, t - 1)

        return carry

    def kv_copy(t, hi, whose):
        k = kv_sems[0] + t * 2 + hi
        return pltpu.make_async_remote_copy(
            src_ref=KV.at[t, hi, whose], dst_ref=KV.at[t, hi, whose],
            send_sem=send_sem.at[k], recv_sem=recv_sem.at[k], device_id=sib, device_id_type=MESH,
        )

    lax.fori_loop(0, HEADS // 2 + 1, chunk, 0)

    slot0 = s * 384

    def norm(user, block):
        rows_a = attn[user, block]
        mean = jnp.sum(rows_a, axis=1, keepdims=True) * (1.0 / 1024)
        centered = rows_a - mean
        var = jnp.sum(centered * centered, axis=1, keepdims=True) * (1.0 / 1024)
        normed = centered * lax.rsqrt(var + 1e-06)
        gated[user, block] = (normed * gate[user, block].astype(F32)).astype(BF16)

    def norm_step(i, carry):
        norm(0, pl.ds(pl.multiple_of(i * 64, 64), 64))
        return carry

    lax.fori_loop(0, 6, norm_step, 0)
    for user in range(users_here):
        for n in range(4):
            ncols = pl.ds(n * 256, 256)
            mixed = jnp.dot(gated[user], ow_v[:, ncols], preferred_element_type=F32)
            mixed = mixed + cand_v[user, :, ncols].astype(F32)
            slot = slot0 + lax.broadcasted_iota(jnp.int32, (384, 256), 0)
            out_v[user, :, ncols] = jnp.where(slot < ccount_ref[user], mixed, 0.0).astype(BF16)
            if user == 0:
                for piece in range(3):
                    norm(1, pl.ds(n * 96 + piece * 32, 32))
        pltpu.make_async_copy(out_v.at[user], out_ref.at[user], local_sem.at[3 + user]).start()
    for user in range(users_here):
        pltpu.make_async_copy(out_v.at[user], out_ref.at[user], local_sem.at[3 + user]).wait()
    for number in range(HEADS):
        kv_copy(number // 2, number % 2, c).wait_send()
    for src, k in sent:
        rcopy(src, src, k, sib).wait_send()
    assert state["k"] <= NSEM


def body(candidates, history, proj_weight, out_weight, hist_len, cand_count):
    anyspace = pl.BlockSpec(memory_space=pl.ANY)
    smem = pl.BlockSpec(memory_space=pltpu.SMEM)
    vmem = pl.BlockSpec(memory_space=pltpu.VMEM)
    return pl.pallas_call(
        kernel,
        out_shape=jax.ShapeDtypeStruct(candidates.shape, BF16),
        in_specs=[anyspace, anyspace, vmem, anyspace, smem, smem],
        out_specs=anyspace,
        scratch_shapes=[
            pltpu.VMEM((2, NX, NY, NZ, 16, 1024), BF16),
            pltpu.VMEM((NX, 2, 2, 32, 1024), BF16),
            pltpu.VMEM((4, 2, 2, 512, 256), BF16),
            pltpu.VMEM((2, 2, 2, 384, 128), BF16),
            pltpu.VMEM((2, 2, 4, 128, 1024), BF16),
            pltpu.VMEM((256, 256), BF16),
            pltpu.VMEM((2, 384, 1024), BF16),
            pltpu.VMEM((1024, 1024), BF16),
            pltpu.VMEM((512, 128), F32),
            pltpu.VMEM((2, 384, 1024), F32),
            pltpu.VMEM((2, 384, 1024), BF16),
            pltpu.VMEM((2, 384, 1024), BF16),
            pltpu.VMEM((2, 384, 1024), BF16),
            pltpu.SemaphoreType.DMA((NSEM,)),
            pltpu.SemaphoreType.DMA((NSEM,)),
            pltpu.SemaphoreType.DMA((5,)),
        ],
        compiler_params=pltpu.CompilerParams(
            collective_id=0, has_side_effects=True, vmem_limit_bytes=56 * 1024 * 1024
        ),
    )(candidates, history, proj_weight, out_weight, hist_len, cand_count)


def solution(mesh):
    in_specs = (
        P("users", "score", None),
        P("users", "score", None),
        P(("users", "score"), None, None),
        P(),
        P("users"),
        P("users"),
    )
    out_specs = P("users", "score", None)
    return jax.shard_map(body, mesh=mesh, in_specs=in_specs, out_specs=out_specs, check_vma=False)
```

```python
import functools
import math

import jax
import jax.numpy as jnp
from jax import lax
from jax.experimental import pallas as pl
from jax.experimental.pallas import tpu as pltpu
from jax.sharding import PartitionSpec as P

MESH = pl.DeviceIdType.MESH
HEADS = 8
NX, NY, NZ = 4, 4, 8
BF16, F32 = jnp.bfloat16, jnp.float32
COLS_X, COLS_Y, COLS_Z = pl.ds(0, 256), pl.ds(256, 384), pl.ds(640, 384)
COLS_XY = pl.ds(0, 640)
SLOT = {0: 0, -1: 1, 1: 2, -2: 3, 2: 4, -3: 5, 3: 6, 4: 7, -4: 7}
NSEM = 128


def nt_dot(a, b):
    return lax.dot_general(a, b, (((1,), (1,)), ((), ())), preferred_element_type=F32)


def half_silu(t):
    return t + t * jnp.tanh(t)


def kernel(
    cand_ref, hist_ref, proj_ref, ow_ref, hlen_ref, ccount_ref, out_ref,
    G, H, KV, Q, W, pick_v, cand_v, ow_v, mask_v, attn, gate, gated, out_v, send_sem, recv_sem, local_sem,
):
    u = lax.axis_index("users")
    s = lax.axis_index("score")
    z = lax.rem(u, NZ)
    yhi = lax.div(u, NZ)
    c = lax.rem(s, 2)
    x = lax.rem(lax.div(s, 2), NX)
    ylo = lax.div(s, 8)
    y = yhi * 2 + ylo
    oc = 1 - c

    def dev(px, py, pz, pc):
        return (lax.div(py, 2) * NZ + pz, lax.rem(py, 2) * 8 + px * 2 + pc)

    def up(pos, n, k):
        return lax.rem(pos + k + n, n)

    yo = y + 1 - 2 * ylo
    sib = dev(x, y, z, oc)
    local = [
        pltpu.make_async_copy(hist_ref.at[c], H.at[x, ylo, c], local_sem.at[0]),
        pltpu.make_async_copy(cand_ref, cand_v, local_sem.at[1]),
        pltpu.make_async_copy(ow_ref, ow_v, local_sem.at[2]),
    ]
    for copy in local:
        copy.start()

    barrier = pltpu.get_barrier_semaphore()
    partners = [dev(up(x, NX, k), y, z, c) for k in (1, 3, 2)] + [dev(x, up(y, NY, k), z, c) for k in (1, 3, 2)]
    partners += [dev(x, y, up(z, NZ, k), c) for k in (1, 7, 2, 6, 3, 5, 4)] + [sib, dev(x, yo, z, oc)]
    for partner in partners:
        pl.semaphore_signal(barrier, inc=1, device_id=partner, device_id_type=MESH)

    row16 = lax.broadcasted_iota(jnp.int32, (16, 1024), 0)
    tile = jnp.zeros((16, 1024), F32)
    for f in range(4):
        rows_f = proj_ref[f].astype(F32)
        for p in range(4):
            tile = jnp.where(row16 == f * 4 + p, jnp.broadcast_to(rows_f[p : p + 1], (16, 1024)), tile)
    G[c, x, y, 0] = tile.astype(BF16)

    pl.semaphore_wait(barrier, len(partners))

    state = {"k": 0}
    sent = []

    def new_sem():
        k = state["k"]
        state["k"] = k + 1
        return k

    def rcopy(src, dst, k, target):
        return pltpu.make_async_remote_copy(
            src_ref=src(), dst_ref=dst(), send_sem=send_sem.at[k], recv_sem=recv_sem.at[k],
            device_id=target, device_id_type=MESH,
        )

    def send(src, dst, k, target):
        rcopy(src, dst, k, target).start()
        sent.append((src, k))

    def wait(dst, k):
        rcopy(dst, dst, k, sib).wait_recv()

    hist_arrivals = []
    for who, target, py, pc in (
        (oc, sib, ylo, oc), (c, dev(x, yo, z, c), 1 - ylo, c), (oc, dev(x, yo, z, oc), 1 - ylo, oc),
    ):
        k = new_sem()
        send(functools.partial(hist_ref.at.__getitem__, who), lambda: H.at[x, ylo, c], k, target)
        hist_arrivals.append((functools.partial(H.at.__getitem__, (x, py, pc)), k))

    whole = slice(None)

    def view(plane, xs, ys, slots, columns):
        return lambda: G.at[plane, xs, ys, slots, :, columns]

    def direct(axis, block):
        n, at = (NX, x) if axis == "x" else (NY, y)
        arrivals = []
        for step in (1, 3, 2):
            k = new_sem()
            to = up(at, n, step)
            send(block(at), block(at), k, dev(to, y, z, c) if axis == "x" else dev(x, to, z, c))
            arrivals.append((block(up(at, n, -step)), k))
        return arrivals

    def settle(arrivals):
        for where, k in arrivals:
            wait(where, k)

    waves = {2: pl.ds(3, 2), 3: pl.ds(5, 2), 4: pl.ds(7, 1)}
    groups = [pl.ds(0, 3), pl.ds(3, 2), pl.ds(5, 3)]

    def second(w):
        group_x = direct("y", lambda at: view(c, x, at, groups[w], COLS_X))
        group_y = direct("x", lambda at: view(c, at, y, groups[w], COLS_Y))
        return group_x, group_y

    def third(w, arrivals):
        settle(arrivals[0])
        group_x = direct("x", lambda at: view(c, at, whole, groups[w], COLS_X))
        settle(arrivals[1])
        group_y = direct("y", lambda at: view(c, whole, at, groups[w], COLS_Y))
        return group_x + group_y

    spot = {"x": [up(x, NX, k) for k in range(NX)], "y": [up(y, NY, k) for k in range(NY)]}
    neighbour = {
        "x": [dev(spot["x"][k], y, z, c) for k in range(NX)],
        "y": [dev(x, spot["y"][k], z, c) for k in range(NY)],
    }

    def ring_plan(axis, block):
        first = [(block(spot[axis][3], None), new_sem()), (block(spot[axis][1], None), new_sem())]
        return first, [(block(spot[axis][2], half), new_sem()) for half in range(2)]

    def ring_first(axis, block, plan):
        for (_, k), step in zip(plan[0], (1, 3)):
            send(block(spot[axis][0], None), block(spot[axis][0], None), k, neighbour[axis][step])

    def ring_second(axis, block, plan):
        settle(plan[0])
        for half, step in ((0, 1), (1, 3)):
            mine = block(spot[axis][4 - step], half)
            send(mine, mine, plan[1][half][1], neighbour[axis][step])

    def part(half):
        return whole if half is None else pl.ds(2 * half, 2)

    def wave_x(w):
        return "x", lambda at, half: view(c, at, part(half), groups[w], COLS_X)

    def wave_y(w):
        return "y", lambda at, half: view(c, part(half), at, groups[w], COLS_Y)

    plans = {w: (ring_plan(*wave_x(w)), ring_plan(*wave_y(w))) for w in (1, 2)}

    def third_first(w):
        settle(stage2[w][0])
        ring_first(*wave_x(w), plans[w][0])
        settle(stage2[w][1])
        ring_first(*wave_y(w), plans[w][1])

    def third_second(w):
        ring_second(*wave_x(w), plans[w][0])
        ring_second(*wave_y(w), plans[w][1])

    def hist_block(at, half):
        return (lambda: H.at[at]) if half is None else (lambda: H.at[at, half])

    hist_plan = ring_plan("x", hist_block)
    along_z = {}

    def z_send(off):
        k = new_sem()
        send(view(c, x, y, 0, COLS_XY), view(c, x, y, SLOT[-off], COLS_XY), k, dev(x, y, up(z, NZ, off), c))
        along_z[SLOT[-off]] = (view(c, x, y, SLOT[-off], COLS_XY), k)

    zx = direct("x", lambda at: view(c, at, y, 0, COLS_Z))
    for off in (1, -1, 2, -2, 3, -3, 4):
        z_send(off)
    settle([along_z[1], along_z[2]])
    stage2 = {0: second(0)}
    settle(zx)
    zy = direct("y", lambda at: view(c, whole, at, 0, COLS_Z))
    settle([along_z[3], along_z[4]])
    stage2[1] = second(1)
    settle(zy)

    z_right, z_left = dev(x, y, up(z, NZ, 1), c), dev(x, y, up(z, NZ, -1), c)
    ring_sems = [(new_sem(), new_sem()) for _ in range(4)]
    first_xy, first_z = new_sem(), new_sem()
    twin_sems = {w: new_sem() for w in (2, 3, 4)}
    kv_sems = [new_sem() for _ in range(HEADS)]

    def ring_blocks(w):
        xs = (whole, whole) if w < 4 else (pl.ds(0, 2), pl.ds(2, 2))
        down, high = (2 * w - 3, 2 * w - 2) if w > 1 else (0, 0)
        into = (2 * w - 1, 2 * w) if w < 4 else (7, 7)
        return [
            (view(c, xs[0], whole, down, COLS_Z), view(c, xs[0], whole, into[0], COLS_Z)),
            (view(c, xs[1], whole, high, COLS_Z), view(c, xs[1], whole, into[1], COLS_Z)),
        ]

    def ring_send(w):
        for (src, dst), k, target in zip(ring_blocks(w), ring_sems[w - 1], (z_right, z_left)):
            send(src, dst, k, target)

    def ring_wait(w):
        for (_, dst), k in zip(ring_blocks(w), ring_sems[w - 1]):
            wait(dst, k)

    def twin_send(w):
        block = view(c, whole, whole, waves[w], whole)
        send(block, block, twin_sems[w], sib)

    def twin_wait(w):
        wait(view(oc, whole, whole, waves[w], whole), twin_sems[w])

    ring_send(1)
    stage3 = third(0, stage2[0])
    local[0].wait()
    settle(hist_arrivals)
    ring_first("x", hist_block, hist_plan)
    settle([along_z[5], along_z[6], along_z[7]])
    stage2[2] = second(2)
    ring_wait(1)
    ring_send(2)
    block = view(c, whole, whole, groups[0], COLS_Z)
    send(block, block, first_z, sib)
    third_first(1)
    settle(stage3)
    block_xy = view(c, whole, whole, groups[0], COLS_XY)
    send(block_xy, block_xy, first_xy, sib)
    ring_second("x", hist_block, hist_plan)
    third_first(2)
    local[1].wait()
    local[2].wait()
    wait(view(oc, whole, whole, groups[0], COLS_Z), first_z)
    wait(view(oc, whole, whole, groups[0], COLS_XY), first_xy)

    head_size = 128
    score_half = 0.5 / math.sqrt(head_size)
    users_here = cand_v.shape[0]

    q = lax.broadcasted_iota(jnp.int32, (512, 128), 0)
    event = (((q >> 6) & 1) * 8 + (q >> 7) * 2 + ((q >> 5) & 1)) * 32 + (q & 31)
    mask_v[...] = (event < hlen_ref[c]).astype(F32)
    out_row = lax.broadcasted_iota(jnp.int32, (256, 256), 0)
    in_row = lax.broadcasted_iota(jnp.int32, (256, 256), 1)
    source = ((out_row & 63) >> 2) * 16 + (out_row & 3) * 4 + (out_row >> 6)
    pick_v[...] = (in_row == source).astype(F32).astype(BF16)

    odd = lax.rem(z, 2)

    def slabs(hi, slot):
        return jnp.concatenate(
            [G[plane, px, hi * 2 + yl, slot] for yl in range(2) for px in range(NX) for plane in range(2)],
            axis=0,
        )

    def choose(t, even_slots, odd_slots):
        slot = jnp.int32(0)
        for number in range(4):
            slot = jnp.where(t == number, jnp.where(odd == 1, odd_slots[number], even_slots[number]), slot)
        return slot

    def pair_of(t):
        turn = t + lax.div(t, 2) - 2 * lax.div(t, 3)
        return lax.rem(lax.div(z, 2) + (2 * odd - 1) * turn + 8, 4)

    def columns_of(t, hi):
        return pl.ds(pl.multiple_of((hi * 4 + pair_of(t)) * 128, 128), 128)

    def project(t, hi):
        slots = (choose(t, (0, 3, 4, 7), (1, 2, 5, 6)), choose(t, (2, 1, 6, 5), (0, 4, 3, 7)))
        keep, at = lax.rem(t, 2), columns_of(t, hi)
        for zl in range(2):
            sorted_rows = jnp.dot(pick_v[...], slabs(hi, slots[zl]), preferred_element_type=F32).astype(BF16)
            for p in range(4):
                W[keep, hi, p, zl * 64 : zl * 64 + 64] = sorted_rows[p * 64 : p * 64 + 64]
        parts = half_silu(0.5 * nt_dot(cand_v[...].reshape(768, 1024), W[keep, hi].reshape(512, 1024))).astype(BF16)
        own_keys, own_values = parts[:, :128], parts[:, 128:256]
        queries, user_gate = parts[:, 256:384], parts[:, 384:]
        own = jnp.dot(queries * own_keys, jnp.ones((128, 128), BF16), preferred_element_type=F32)
        own = half_silu(own * score_half) * own_values.astype(F32)
        for user in range(users_here):
            rows_u = slice(user * 384, user * 384 + 384)
            Q[keep, hi, user] = queries[rows_u]
            gate[user, :, at] = user_gate[rows_u]
            attn[user, :, at] = own[rows_u]

    def keys_values(t, hi):
        w_kv = W[lax.rem(t, 2), hi, 0:2].reshape(256, 1024)
        kv = half_silu(0.5 * nt_dot(H[...].reshape(512, 1024), w_kv))
        KV[t, hi, c, :, :128] = kv[:, :128].astype(BF16)
        KV[t, hi, c, :, 128:] = (kv[:, 128:] * mask_v[...]).astype(BF16)
        kv_copy(t, hi, c).start()

    def attend(t, hi):
        kv_copy(t, hi, oc).wait_recv()
        keep, at = lax.rem(t, 2), columns_of(t, hi)
        for user in range(users_here):
            keys, values = KV[t, hi, user, :, :128], KV[t, hi, user, :, 128:]
            weights = half_silu(nt_dot(Q[keep, hi, user], keys) * score_half).astype(BF16)
            attn[user, :, at] += jnp.dot(weights, values, preferred_element_type=F32)

    def both(work, t):
        def step(hi, carry):
            work(t, hi)
            return carry

        lax.fori_loop(0, 2, step, 0)

    def chunk(t, carry):
        @pl.when(t == 1)
        def _():
            settle(hist_plan[1])

        @pl.when(t > 0)
        def _():
            both(keys_values, t - 1)

        for w in (2, 3, 4):
            @pl.when(t == w - 1)
            def _():
                twin_wait(w)

        @pl.when(t < 4)
        def _():
            both(project, t)

        def forward(w):
            ring_wait(w)
            if w < 4:
                ring_send(w + 1)
            if w == 2:
                third_second(1)
                settle(plans[1][0][1] + plans[1][1][1])
            if w == 3:
                settle(plans[2][0][1] + plans[2][1][1])
            twin_send(w)
            if w == 2:
                third_second(2)

        @pl.when(t == 0)
        def _():
            forward(2)

        @pl.when(t > 0)
        def _():
            attend(t - 1, 0)

        for w in (3, 4):
            @pl.when(t == w - 2)
            def _():
                forward(w)

        @pl.when(t > 0)
        def _():
            attend(t - 1, 1)

        return carry

    def kv_copy(t, hi, whose):
        k = kv_sems[0] + t * 2 + hi
        return pltpu.make_async_remote_copy(
            src_ref=KV.at[t, hi, whose], dst_ref=KV.at[t, hi, whose],
            send_sem=send_sem.at[k], recv_sem=recv_sem.at[k], device_id=sib, device_id_type=MESH,
        )

    lax.fori_loop(0, HEADS // 2 + 1, chunk, 0)

    slot0 = s * 384

    def norm(user, block):
        rows_a = attn[user, block]
        mean = jnp.sum(rows_a, axis=1, keepdims=True) * (1.0 / 1024)
        centered = rows_a - mean
        var = jnp.sum(centered * centered, axis=1, keepdims=True) * (1.0 / 1024)
        normed = centered * lax.rsqrt(var + 1e-06)
        gated[user, block] = (normed * gate[user, block].astype(F32)).astype(BF16)

    def norm_step(i, carry):
        norm(0, pl.ds(pl.multiple_of(i * 64, 64), 64))
        return carry

    lax.fori_loop(0, 6, norm_step, 0)
    for user in range(users_here):
        for n in range(4):
            ncols = pl.ds(n * 256, 256)
            mixed = jnp.dot(gated[user], ow_v[:, ncols], preferred_element_type=F32)
            mixed = mixed + cand_v[user, :, ncols].astype(F32)
            slot = slot0 + lax.broadcasted_iota(jnp.int32, (384, 256), 0)
            out_v[user, :, ncols] = jnp.where(slot < ccount_ref[user], mixed, 0.0).astype(BF16)
            if user == 0:
                for piece in range(3):
                    norm(1, pl.ds(n * 96 + piece * 32, 32))
        pltpu.make_async_copy(out_v.at[user], out_ref.at[user], local_sem.at[3 + user]).start()
    for user in range(users_here):
        pltpu.make_async_copy(out_v.at[user], out_ref.at[user], local_sem.at[3 + user]).wait()
    for number in range(HEADS):
        kv_copy(number // 2, number % 2, c).wait_send()
    for src, k in sent:
        rcopy(src, src, k, sib).wait_send()
    assert state["k"] <= NSEM


def body(candidates, history, proj_weight, out_weight, hist_len, cand_count):
    anyspace = pl.BlockSpec(memory_space=pl.ANY)
    smem = pl.BlockSpec(memory_space=pltpu.SMEM)
    vmem = pl.BlockSpec(memory_space=pltpu.VMEM)
    return pl.pallas_call(
        kernel,
        out_shape=jax.ShapeDtypeStruct(candidates.shape, BF16),
        in_specs=[anyspace, anyspace, vmem, anyspace, smem, smem],
        out_specs=anyspace,
        scratch_shapes=[
            pltpu.VMEM((2, NX, NY, NZ, 16, 1024), BF16),
            pltpu.VMEM((NX, 2, 2, 32, 1024), BF16),
            pltpu.VMEM((4, 2, 2, 512, 256), BF16),
            pltpu.VMEM((2, 2, 2, 384, 128), BF16),
            pltpu.VMEM((2, 2, 4, 128, 1024), BF16),
            pltpu.VMEM((256, 256), BF16),
            pltpu.VMEM((2, 384, 1024), BF16),
            pltpu.VMEM((1024, 1024), BF16),
            pltpu.VMEM((512, 128), F32),
            pltpu.VMEM((2, 384, 1024), F32),
            pltpu.VMEM((2, 384, 1024), BF16),
            pltpu.VMEM((2, 384, 1024), BF16),
            pltpu.VMEM((2, 384, 1024), BF16),
            pltpu.SemaphoreType.DMA((NSEM,)),
            pltpu.SemaphoreType.DMA((NSEM,)),
            pltpu.SemaphoreType.DMA((5,)),
        ],
        compiler_params=pltpu.CompilerParams(
            collective_id=0, has_side_effects=True, vmem_limit_bytes=56 * 1024 * 1024
        ),
    )(candidates, history, proj_weight, out_weight, hist_len, cand_count)


def solution(mesh):
    in_specs = (
        P("users", "score", None),
        P("users", "score", None),
        P(("users", "score"), None, None),
        P(),
        P("users"),
        P("users"),
    )
    out_specs = P("users", "score", None)
    return jax.shard_map(body, mesh=mesh, in_specs=in_specs, out_specs=out_specs, check_vma=False)
```

```python
import functools
import math

import jax
import jax.numpy as jnp
from jax import lax
from jax.experimental import pallas as pl
from jax.experimental.pallas import tpu as pltpu
from jax.sharding import PartitionSpec as P

MESH = pl.DeviceIdType.MESH
HEADS = 8
NX, NY, NZ = 4, 4, 8
BF16, F32 = jnp.bfloat16, jnp.float32
COLS_X, COLS_Y, COLS_Z = pl.ds(0, 256), pl.ds(256, 384), pl.ds(640, 384)
COLS_XY = pl.ds(0, 640)
SLOT = {0: 0, -1: 1, 1: 2, -2: 3, 2: 4, -3: 5, 3: 6, 4: 7, -4: 7}
NSEM = 128


def nt_dot(a, b):
    return lax.dot_general(a, b, (((1,), (1,)), ((), ())), preferred_element_type=F32)


def half_silu(t):
    return t + t * jnp.tanh(t)


def kernel(
    cand_ref, hist_ref, proj_ref, ow_ref, hlen_ref, ccount_ref, out_ref,
    G, H, KV, Q, W, pick_v, cand_v, ow_v, mask_v, attn, gate, gated, out_v, send_sem, recv_sem, local_sem,
):
    u = lax.axis_index("users")
    s = lax.axis_index("score")
    z = lax.rem(u, NZ)
    yhi = lax.div(u, NZ)
    c = lax.rem(s, 2)
    x = lax.rem(lax.div(s, 2), NX)
    ylo = lax.div(s, 8)
    y = yhi * 2 + ylo
    oc = 1 - c

    def dev(px, py, pz, pc):
        return (lax.div(py, 2) * NZ + pz, lax.rem(py, 2) * 8 + px * 2 + pc)

    def up(pos, n, k):
        return lax.rem(pos + k + n, n)

    yo = y + 1 - 2 * ylo
    sib = dev(x, y, z, oc)
    local = [
        pltpu.make_async_copy(hist_ref.at[c], H.at[x, ylo, c], local_sem.at[0]),
        pltpu.make_async_copy(cand_ref, cand_v, local_sem.at[1]),
        pltpu.make_async_copy(ow_ref, ow_v, local_sem.at[2]),
    ]
    for copy in local:
        copy.start()

    barrier = pltpu.get_barrier_semaphore()
    partners = [dev(up(x, NX, k), y, z, c) for k in (1, 3, 2)] + [dev(x, up(y, NY, k), z, c) for k in (1, 3, 2)]
    partners += [dev(x, y, up(z, NZ, k), c) for k in (1, 7, 2, 6, 3, 5, 4)] + [sib, dev(x, yo, z, oc)]
    for partner in partners:
        pl.semaphore_signal(barrier, inc=1, device_id=partner, device_id_type=MESH)

    row16 = lax.broadcasted_iota(jnp.int32, (16, 1024), 0)
    tile = jnp.zeros((16, 1024), F32)
    for f in range(4):
        rows_f = proj_ref[f].astype(F32)
        for p in range(4):
            tile = jnp.where(row16 == f * 4 + p, jnp.broadcast_to(rows_f[p : p + 1], (16, 1024)), tile)
    G[c, x, y, 0] = tile.astype(BF16)

    pl.semaphore_wait(barrier, len(partners))

    state = {"k": 0}
    sent = []

    def new_sem():
        k = state["k"]
        state["k"] = k + 1
        return k

    def rcopy(src, dst, k, target):
        return pltpu.make_async_remote_copy(
            src_ref=src(), dst_ref=dst(), send_sem=send_sem.at[k], recv_sem=recv_sem.at[k],
            device_id=target, device_id_type=MESH,
        )

    def send(src, dst, k, target):
        rcopy(src, dst, k, target).start()
        sent.append((src, k))

    def wait(dst, k):
        rcopy(dst, dst, k, sib).wait_recv()

    hist_arrivals = []
    for who, target, py, pc in (
        (oc, sib, ylo, oc), (c, dev(x, yo, z, c), 1 - ylo, c), (oc, dev(x, yo, z, oc), 1 - ylo, oc),
    ):
        k = new_sem()
        send(functools.partial(hist_ref.at.__getitem__, who), lambda: H.at[x, ylo, c], k, target)
        hist_arrivals.append((functools.partial(H.at.__getitem__, (x, py, pc)), k))

    whole = slice(None)

    def view(plane, xs, ys, slots, columns):
        return lambda: G.at[plane, xs, ys, slots, :, columns]

    def direct(axis, block):
        n, at = (NX, x) if axis == "x" else (NY, y)
        arrivals = []
        for step in (1, 3, 2):
            k = new_sem()
            to = up(at, n, step)
            send(block(at), block(at), k, dev(to, y, z, c) if axis == "x" else dev(x, to, z, c))
            arrivals.append((block(up(at, n, -step)), k))
        return arrivals

    def settle(arrivals):
        for where, k in arrivals:
            wait(where, k)

    waves = {2: pl.ds(3, 2), 3: pl.ds(5, 2), 4: pl.ds(7, 1)}
    groups = [pl.ds(0, 3), pl.ds(3, 2), pl.ds(5, 3)]

    def second(w):
        group_x = direct("y", lambda at: view(c, x, at, groups[w], COLS_X))
        group_y = direct("x", lambda at: view(c, at, y, groups[w], COLS_Y))
        return group_x, group_y

    def third(w, arrivals):
        settle(arrivals[0])
        group_x = direct("x", lambda at: view(c, at, whole, groups[w], COLS_X))
        settle(arrivals[1])
        group_y = direct("y", lambda at: view(c, whole, at, groups[w], COLS_Y))
        return group_x + group_y

    spot = {"x": [up(x, NX, k) for k in range(NX)], "y": [up(y, NY, k) for k in range(NY)]}
    neighbour = {
        "x": [dev(spot["x"][k], y, z, c) for k in range(NX)],
        "y": [dev(x, spot["y"][k], z, c) for k in range(NY)],
    }

    def ring_plan(axis, block):
        first = [(block(spot[axis][3], None), new_sem()), (block(spot[axis][1], None), new_sem())]
        return first, [(block(spot[axis][2], half), new_sem()) for half in range(2)]

    def ring_first(axis, block, plan):
        for (_, k), step in zip(plan[0], (1, 3)):
            send(block(spot[axis][0], None), block(spot[axis][0], None), k, neighbour[axis][step])

    def ring_second(axis, block, plan):
        settle(plan[0])
        for half, step in ((0, 1), (1, 3)):
            mine = block(spot[axis][4 - step], half)
            send(mine, mine, plan[1][half][1], neighbour[axis][step])

    def hist_block(at, half):
        return (lambda: H.at[at]) if half is None else (lambda: H.at[at, half])

    hist_plan = ring_plan("x", hist_block)
    along_z = {}

    def z_send(off):
        k = new_sem()
        send(view(c, x, y, 0, COLS_XY), view(c, x, y, SLOT[-off], COLS_XY), k, dev(x, y, up(z, NZ, off), c))
        along_z[SLOT[-off]] = (view(c, x, y, SLOT[-off], COLS_XY), k)

    zx = direct("x", lambda at: view(c, at, y, 0, COLS_Z))
    for off in (1, -1, 2, -2, 3, -3, 4):
        z_send(off)
    settle([along_z[1], along_z[2]])
    stage2 = {0: second(0)}
    settle(zx)
    zy = direct("y", lambda at: view(c, whole, at, 0, COLS_Z))
    settle([along_z[3], along_z[4]])
    stage2[1] = second(1)
    settle(zy)

    z_right, z_left = dev(x, y, up(z, NZ, 1), c), dev(x, y, up(z, NZ, -1), c)
    ring_sems = [(new_sem(), new_sem()) for _ in range(4)]
    first_xy, first_z = new_sem(), new_sem()
    twin_sems = {w: new_sem() for w in (2, 3, 4)}
    kv_sems = [new_sem() for _ in range(HEADS)]

    def ring_blocks(w):
        xs = (whole, whole) if w < 4 else (pl.ds(0, 2), pl.ds(2, 2))
        down, high = (2 * w - 3, 2 * w - 2) if w > 1 else (0, 0)
        into = (2 * w - 1, 2 * w) if w < 4 else (7, 7)
        return [
            (view(c, xs[0], whole, down, COLS_Z), view(c, xs[0], whole, into[0], COLS_Z)),
            (view(c, xs[1], whole, high, COLS_Z), view(c, xs[1], whole, into[1], COLS_Z)),
        ]

    def ring_send(w):
        for (src, dst), k, target in zip(ring_blocks(w), ring_sems[w - 1], (z_right, z_left)):
            send(src, dst, k, target)

    def ring_wait(w):
        for (_, dst), k in zip(ring_blocks(w), ring_sems[w - 1]):
            wait(dst, k)

    def twin_send(w):
        block = view(c, whole, whole, waves[w], whole)
        send(block, block, twin_sems[w], sib)

    def twin_wait(w):
        wait(view(oc, whole, whole, waves[w], whole), twin_sems[w])

    ring_send(1)
    stage3 = third(0, stage2[0])
    local[0].wait()
    settle(hist_arrivals)
    ring_first("x", hist_block, hist_plan)
    settle([along_z[5], along_z[6], along_z[7]])
    stage2[2] = second(2)
    ring_wait(1)
    ring_send(2)
    block = view(c, whole, whole, groups[0], COLS_Z)
    send(block, block, first_z, sib)
    later = {1: third(1, stage2[1])}
    settle(stage3)
    block_xy = view(c, whole, whole, groups[0], COLS_XY)
    send(block_xy, block_xy, first_xy, sib)
    ring_second("x", hist_block, hist_plan)
    later[2] = third(2, stage2[2])
    local[1].wait()
    local[2].wait()
    wait(view(oc, whole, whole, groups[0], COLS_Z), first_z)
    wait(view(oc, whole, whole, groups[0], COLS_XY), first_xy)

    head_size = 128
    score_half = 0.5 / math.sqrt(head_size)
    users_here = cand_v.shape[0]

    q = lax.broadcasted_iota(jnp.int32, (512, 128), 0)
    event = (((q >> 6) & 1) * 8 + (q >> 7) * 2 + ((q >> 5) & 1)) * 32 + (q & 31)
    mask_v[...] = (event < hlen_ref[c]).astype(F32)
    out_row = lax.broadcasted_iota(jnp.int32, (256, 256), 0)
    in_row = lax.broadcasted_iota(jnp.int32, (256, 256), 1)
    source = ((out_row & 63) >> 2) * 16 + (out_row & 3) * 4 + (out_row >> 6)
    pick_v[...] = (in_row == source).astype(F32).astype(BF16)

    odd = lax.rem(z, 2)

    def slabs(hi, slot):
        return jnp.concatenate(
            [G[plane, px, hi * 2 + yl, slot] for yl in range(2) for px in range(NX) for plane in range(2)],
            axis=0,
        )

    def choose(t, even_slots, odd_slots):
        slot = jnp.int32(0)
        for number in range(4):
            slot = jnp.where(t == number, jnp.where(odd == 1, odd_slots[number], even_slots[number]), slot)
        return slot

    def pair_of(t):
        turn = t + lax.div(t, 2) - 2 * lax.div(t, 3)
        return lax.rem(lax.div(z, 2) + (2 * odd - 1) * turn + 8, 4)

    def columns_of(t, hi):
        return pl.ds(pl.multiple_of((hi * 4 + pair_of(t)) * 128, 128), 128)

    def project(t, hi):
        slots = (choose(t, (0, 3, 4, 7), (1, 2, 5, 6)), choose(t, (2, 1, 6, 5), (0, 4, 3, 7)))
        keep, at = lax.rem(t, 2), columns_of(t, hi)
        for zl in range(2):
            sorted_rows = jnp.dot(pick_v[...], slabs(hi, slots[zl]), preferred_element_type=F32).astype(BF16)
            for p in range(4):
                W[keep, hi, p, zl * 64 : zl * 64 + 64] = sorted_rows[p * 64 : p * 64 + 64]
        parts = half_silu(0.5 * nt_dot(cand_v[...].reshape(768, 1024), W[keep, hi].reshape(512, 1024))).astype(BF16)
        own_keys, own_values = parts[:, :128], parts[:, 128:256]
        queries, user_gate = parts[:, 256:384], parts[:, 384:]
        own = jnp.dot(queries * own_keys, jnp.ones((128, 128), BF16), preferred_element_type=F32)
        own = half_silu(own * score_half) * own_values.astype(F32)
        for user in range(users_here):
            rows_u = slice(user * 384, user * 384 + 384)
            Q[keep, hi, user] = queries[rows_u]
            gate[user, :, at] = user_gate[rows_u]
            attn[user, :, at] = own[rows_u]

    def keys_values(t, hi):
        w_kv = W[lax.rem(t, 2), hi, 0:2].reshape(256, 1024)
        kv = half_silu(0.5 * nt_dot(H[...].reshape(512, 1024), w_kv))
        KV[t, hi, c, :, :128] = kv[:, :128].astype(BF16)
        KV[t, hi, c, :, 128:] = (kv[:, 128:] * mask_v[...]).astype(BF16)
        kv_copy(t, hi, c).start()

    def attend(t, hi):
        kv_copy(t, hi, oc).wait_recv()
        keep, at = lax.rem(t, 2), columns_of(t, hi)
        for user in range(users_here):
            keys, values = KV[t, hi, user, :, :128], KV[t, hi, user, :, 128:]
            weights = half_silu(nt_dot(Q[keep, hi, user], keys) * score_half).astype(BF16)
            attn[user, :, at] += jnp.dot(weights, values, preferred_element_type=F32)

    def both(work, t):
        def step(hi, carry):
            work(t, hi)
            return carry

        lax.fori_loop(0, 2, step, 0)

    def chunk(t, carry):
        @pl.when(t == 1)
        def _():
            settle(hist_plan[1])

        @pl.when(t > 0)
        def _():
            both(keys_values, t - 1)
            both(attend, t - 1)

        for w in (2, 3, 4):
            @pl.when(t == w - 1)
            def _():
                twin_wait(w)

        @pl.when(t < 4)
        def _():
            both(project, t)

        def forward(w):
            ring_wait(w)
            if w < 4:
                ring_send(w + 1)
            if w < 4:
                settle(later[w - 1])
            twin_send(w)

        for w in (2, 3, 4):
            @pl.when(t == w - 2)
            def _():
                forward(w)

        return carry

    def kv_copy(t, hi, whose):
        k = kv_sems[0] + t * 2 + hi
        return pltpu.make_async_remote_copy(
            src_ref=KV.at[t, hi, whose], dst_ref=KV.at[t, hi, whose],
            send_sem=send_sem.at[k], recv_sem=recv_sem.at[k], device_id=sib, device_id_type=MESH,
        )

    lax.fori_loop(0, HEADS // 2 + 1, chunk, 0)

    slot0 = s * 384

    def norm(user, block):
        rows_a = attn[user, block]
        mean = jnp.sum(rows_a, axis=1, keepdims=True) * (1.0 / 1024)
        centered = rows_a - mean
        var = jnp.sum(centered * centered, axis=1, keepdims=True) * (1.0 / 1024)
        normed = centered * lax.rsqrt(var + 1e-06)
        gated[user, block] = (normed * gate[user, block].astype(F32)).astype(BF16)

    def norm_step(i, carry):
        norm(0, pl.ds(pl.multiple_of(i * 64, 64), 64))
        return carry

    lax.fori_loop(0, 6, norm_step, 0)
    for user in range(users_here):
        for n in range(4):
            ncols = pl.ds(n * 256, 256)
            mixed = jnp.dot(gated[user], ow_v[:, ncols], preferred_element_type=F32)
            mixed = mixed + cand_v[user, :, ncols].astype(F32)
            slot = slot0 + lax.broadcasted_iota(jnp.int32, (384, 256), 0)
            out_v[user, :, ncols] = jnp.where(slot < ccount_ref[user], mixed, 0.0).astype(BF16)
            if user == 0:
                for piece in range(3):
                    norm(1, pl.ds(n * 96 + piece * 32, 32))
        pltpu.make_async_copy(out_v.at[user], out_ref.at[user], local_sem.at[3 + user]).start()
    for user in range(users_here):
        pltpu.make_async_copy(out_v.at[user], out_ref.at[user], local_sem.at[3 + user]).wait()
    for number in range(HEADS):
        kv_copy(number // 2, number % 2, c).wait_send()
    for src, k in sent:
        rcopy(src, src, k, sib).wait_send()
    assert state["k"] <= NSEM


def body(candidates, history, proj_weight, out_weight, hist_len, cand_count):
    anyspace = pl.BlockSpec(memory_space=pl.ANY)
    smem = pl.BlockSpec(memory_space=pltpu.SMEM)
    vmem = pl.BlockSpec(memory_space=pltpu.VMEM)
    return pl.pallas_call(
        kernel,
        out_shape=jax.ShapeDtypeStruct(candidates.shape, BF16),
        in_specs=[anyspace, anyspace, vmem, anyspace, smem, smem],
        out_specs=anyspace,
        scratch_shapes=[
            pltpu.VMEM((2, NX, NY, NZ, 16, 1024), BF16),
            pltpu.VMEM((NX, 2, 2, 32, 1024), BF16),
            pltpu.VMEM((4, 2, 2, 512, 256), BF16),
            pltpu.VMEM((2, 2, 2, 384, 128), BF16),
            pltpu.VMEM((2, 2, 4, 128, 1024), BF16),
            pltpu.VMEM((256, 256), BF16),
            pltpu.VMEM((2, 384, 1024), BF16),
            pltpu.VMEM((1024, 1024), BF16),
            pltpu.VMEM((512, 128), F32),
            pltpu.VMEM((2, 384, 1024), F32),
            pltpu.VMEM((2, 384, 1024), BF16),
            pltpu.VMEM((2, 384, 1024), BF16),
            pltpu.VMEM((2, 384, 1024), BF16),
            pltpu.SemaphoreType.DMA((NSEM,)),
            pltpu.SemaphoreType.DMA((NSEM,)),
            pltpu.SemaphoreType.DMA((5,)),
        ],
        compiler_params=pltpu.CompilerParams(
            collective_id=0, has_side_effects=True, vmem_limit_bytes=56 * 1024 * 1024
        ),
    )(candidates, history, proj_weight, out_weight, hist_len, cand_count)


def solution(mesh):
    in_specs = (
        P("users", "score", None),
        P("users", "score", None),
        P(("users", "score"), None, None),
        P(),
        P("users"),
        P("users"),
    )
    out_specs = P("users", "score", None)
    return jax.shard_map(body, mesh=mesh, in_specs=in_specs, out_specs=out_specs, check_vma=False)
```

```python
import functools
import math

import jax
import jax.numpy as jnp
from jax import lax
from jax.experimental import pallas as pl
from jax.experimental.pallas import tpu as pltpu
from jax.sharding import PartitionSpec as P

MESH = pl.DeviceIdType.MESH
HEADS = 8
NX, NY, NZ = 4, 4, 8
BF16, F32 = jnp.bfloat16, jnp.float32
COLS_X, COLS_Y, COLS_Z = pl.ds(0, 256), pl.ds(256, 384), pl.ds(640, 384)
COLS_XY = pl.ds(0, 640)
SLOT = {0: 0, -1: 1, 1: 2, -2: 3, 2: 4, -3: 5, 3: 6, 4: 7, -4: 7}
NSEM = 128


def nt_dot(a, b):
    return lax.dot_general(a, b, (((1,), (1,)), ((), ())), preferred_element_type=F32)


def half_silu(t):
    return t + t * jnp.tanh(t)


def kernel(
    cand_ref, hist_ref, proj_ref, ow_ref, hlen_ref, ccount_ref, out_ref,
    G, H, KV, Q, W, pick_v, cand_v, ow_v, mask_v, attn, gate, gated, out_v, send_sem, recv_sem, local_sem,
):
    u = lax.axis_index("users")
    s = lax.axis_index("score")
    z = lax.rem(u, NZ)
    yhi = lax.div(u, NZ)
    c = lax.rem(s, 2)
    x = lax.rem(lax.div(s, 2), NX)
    ylo = lax.div(s, 8)
    y = yhi * 2 + ylo
    oc = 1 - c

    def dev(px, py, pz, pc):
        return (lax.div(py, 2) * NZ + pz, lax.rem(py, 2) * 8 + px * 2 + pc)

    def up(pos, n, k):
        return lax.rem(pos + k + n, n)

    yo = y + 1 - 2 * ylo
    sib = dev(x, y, z, oc)
    local = [
        pltpu.make_async_copy(hist_ref.at[c], H.at[x, ylo, c], local_sem.at[0]),
        pltpu.make_async_copy(cand_ref, cand_v, local_sem.at[1]),
        pltpu.make_async_copy(ow_ref, ow_v, local_sem.at[2]),
    ]
    for copy in local:
        copy.start()

    barrier = pltpu.get_barrier_semaphore()
    partners = [dev(up(x, NX, k), y, z, c) for k in (1, 3, 2)] + [dev(x, up(y, NY, k), z, c) for k in (1, 3, 2)]
    partners += [dev(x, y, up(z, NZ, k), c) for k in (1, 7, 2, 6, 3, 5, 4)] + [sib, dev(x, yo, z, oc)]
    for partner in partners:
        pl.semaphore_signal(barrier, inc=1, device_id=partner, device_id_type=MESH)

    row16 = lax.broadcasted_iota(jnp.int32, (16, 1024), 0)
    tile = jnp.zeros((16, 1024), F32)
    for f in range(4):
        rows_f = proj_ref[f].astype(F32)
        for p in range(4):
            tile = jnp.where(row16 == f * 4 + p, jnp.broadcast_to(rows_f[p : p + 1], (16, 1024)), tile)
    G[c, x, y, 0] = tile.astype(BF16)

    pl.semaphore_wait(barrier, len(partners))

    state = {"k": 0}
    sent = []

    def new_sem():
        k = state["k"]
        state["k"] = k + 1
        return k

    def rcopy(src, dst, k, target):
        return pltpu.make_async_remote_copy(
            src_ref=src(), dst_ref=dst(), send_sem=send_sem.at[k], recv_sem=recv_sem.at[k],
            device_id=target, device_id_type=MESH,
        )

    def send(src, dst, k, target):
        rcopy(src, dst, k, target).start()
        sent.append((src, k))

    def wait(dst, k):
        rcopy(dst, dst, k, sib).wait_recv()

    hist_arrivals = []
    for who, target, py, pc in (
        (oc, sib, ylo, oc), (c, dev(x, yo, z, c), 1 - ylo, c), (oc, dev(x, yo, z, oc), 1 - ylo, oc),
    ):
        k = new_sem()
        send(functools.partial(hist_ref.at.__getitem__, who), lambda: H.at[x, ylo, c], k, target)
        hist_arrivals.append((functools.partial(H.at.__getitem__, (x, py, pc)), k))

    whole = slice(None)

    def view(plane, xs, ys, slots, columns):
        return lambda: G.at[plane, xs, ys, slots, :, columns]

    def direct(axis, block):
        n, at = (NX, x) if axis == "x" else (NY, y)
        arrivals = []
        for step in (1, 3, 2):
            k = new_sem()
            to = up(at, n, step)
            send(block(at), block(at), k, dev(to, y, z, c) if axis == "x" else dev(x, to, z, c))
            arrivals.append((block(up(at, n, -step)), k))
        return arrivals

    def settle(arrivals):
        for where, k in arrivals:
            wait(where, k)

    waves = {2: pl.ds(3, 2), 3: pl.ds(5, 2), 4: pl.ds(7, 1)}
    groups = [pl.ds(0, 3), pl.ds(3, 2), pl.ds(5, 3)]

    def second(w):
        group_x = direct("y", lambda at: view(c, x, at, groups[w], COLS_X))
        group_y = direct("x", lambda at: view(c, at, y, groups[w], COLS_Y))
        return group_x, group_y

    def third(w, arrivals):
        settle(arrivals[0])
        group_x = direct("x", lambda at: view(c, at, whole, groups[w], COLS_X))
        settle(arrivals[1])
        group_y = direct("y", lambda at: view(c, whole, at, groups[w], COLS_Y))
        return group_x + group_y

    spot = {"x": [up(x, NX, k) for k in range(NX)], "y": [up(y, NY, k) for k in range(NY)]}
    neighbour = {
        "x": [dev(spot["x"][k], y, z, c) for k in range(NX)],
        "y": [dev(x, spot["y"][k], z, c) for k in range(NY)],
    }

    def ring_plan(axis, block):
        first = [(block(spot[axis][3], None), new_sem()), (block(spot[axis][1], None), new_sem())]
        return first, [(block(spot[axis][2], half), new_sem()) for half in range(2)]

    def ring_first(axis, block, plan):
        for (_, k), step in zip(plan[0], (1, 3)):
            send(block(spot[axis][0], None), block(spot[axis][0], None), k, neighbour[axis][step])

    def ring_second(axis, block, plan):
        settle(plan[0])
        for half, step in ((0, 1), (1, 3)):
            mine = block(spot[axis][4 - step], half)
            send(mine, mine, plan[1][half][1], neighbour[axis][step])

    def hist_block(at, half):
        return (lambda: H.at[at]) if half is None else (lambda: H.at[at, half])

    hist_plan = ring_plan("x", hist_block)
    along_z = {}

    def z_send(off):
        k = new_sem()
        send(view(c, x, y, 0, COLS_XY), view(c, x, y, SLOT[-off], COLS_XY), k, dev(x, y, up(z, NZ, off), c))
        along_z[SLOT[-off]] = (view(c, x, y, SLOT[-off], COLS_XY), k)

    zx = direct("x", lambda at: view(c, at, y, 0, COLS_Z))
    for off in (1, -1, 2, -2, 3, -3, 4):
        z_send(off)
    settle([along_z[1], along_z[2]])
    stage2 = {0: second(0)}
    settle(zx)
    zy = direct("y", lambda at: view(c, whole, at, 0, COLS_Z))
    settle([along_z[3], along_z[4]])
    stage2[1] = second(1)
    settle(zy)

    z_right, z_left = dev(x, y, up(z, NZ, 1), c), dev(x, y, up(z, NZ, -1), c)
    ring_sems = [(new_sem(), new_sem()) for _ in range(4)]
    first_xy, first_z = new_sem(), new_sem()
    twin_sems = {w: new_sem() for w in (2, 3, 4)}
    kv_sems = [new_sem() for _ in range(HEADS)]

    def ring_blocks(w):
        xs = (whole, whole) if w < 4 else (pl.ds(0, 2), pl.ds(2, 2))
        down, high = (2 * w - 3, 2 * w - 2) if w > 1 else (0, 0)
        into = (2 * w - 1, 2 * w) if w < 4 else (7, 7)
        return [
            (view(c, xs[0], whole, down, COLS_Z), view(c, xs[0], whole, into[0], COLS_Z)),
            (view(c, xs[1], whole, high, COLS_Z), view(c, xs[1], whole, into[1], COLS_Z)),
        ]

    def ring_send(w):
        for (src, dst), k, target in zip(ring_blocks(w), ring_sems[w - 1], (z_right, z_left)):
            send(src, dst, k, target)

    def ring_wait(w):
        for (_, dst), k in zip(ring_blocks(w), ring_sems[w - 1]):
            wait(dst, k)

    def twin_send(w):
        block = view(c, whole, whole, waves[w], whole)
        send(block, block, twin_sems[w], sib)

    def twin_wait(w):
        wait(view(oc, whole, whole, waves[w], whole), twin_sems[w])

    ring_send(1)
    stage3 = third(0, stage2[0])
    local[0].wait()
    settle(hist_arrivals)
    ring_first("x", hist_block, hist_plan)
    settle([along_z[5], along_z[6], along_z[7]])
    stage2[2] = second(2)
    ring_wait(1)
    ring_send(2)
    block = view(c, whole, whole, groups[0], COLS_Z)
    send(block, block, first_z, sib)
    later = {1: third(1, stage2[1])}
    settle(stage3)
    block_xy = view(c, whole, whole, groups[0], COLS_XY)
    send(block_xy, block_xy, first_xy, sib)
    ring_second("x", hist_block, hist_plan)
    later[2] = third(2, stage2[2])
    local[1].wait()
    local[2].wait()
    wait(view(oc, whole, whole, groups[0], COLS_Z), first_z)
    wait(view(oc, whole, whole, groups[0], COLS_XY), first_xy)

    head_size = 128
    score_half = 0.5 / math.sqrt(head_size)
    users_here = cand_v.shape[0]

    q = lax.broadcasted_iota(jnp.int32, (512, 128), 0)
    event = (((q >> 6) & 1) * 8 + (q >> 7) * 2 + ((q >> 5) & 1)) * 32 + (q & 31)
    mask_v[...] = (event < hlen_ref[c]).astype(F32)
    out_row = lax.broadcasted_iota(jnp.int32, (256, 256), 0)
    in_row = lax.broadcasted_iota(jnp.int32, (256, 256), 1)
    source = ((out_row & 63) >> 2) * 16 + (out_row & 3) * 4 + (out_row >> 6)
    pick_v[...] = (in_row == source).astype(F32).astype(BF16)

    odd = lax.rem(z, 2)

    def slabs(hi, slot):
        return jnp.concatenate(
            [G[plane, px, hi * 2 + yl, slot] for yl in range(2) for px in range(NX) for plane in range(2)],
            axis=0,
        )

    def choose(t, even_slots, odd_slots):
        slot = jnp.int32(0)
        for number in range(4):
            slot = jnp.where(t == number, jnp.where(odd == 1, odd_slots[number], even_slots[number]), slot)
        return slot

    def pair_of(t):
        turn = t + lax.div(t, 2) - 2 * lax.div(t, 3)
        return lax.rem(lax.div(z, 2) + (2 * odd - 1) * turn + 8, 4)

    def columns_of(t, hi):
        return pl.ds(pl.multiple_of((hi * 4 + pair_of(t)) * 128, 128), 128)

    def project(t, hi):
        slots = (choose(t, (0, 3, 4, 7), (1, 2, 5, 6)), choose(t, (2, 1, 6, 5), (0, 4, 3, 7)))
        keep, at = lax.rem(t, 2), columns_of(t, hi)
        for zl in range(2):
            sorted_rows = jnp.dot(pick_v[...], slabs(hi, slots[zl]), preferred_element_type=F32).astype(BF16)
            for p in range(4):
                W[keep, hi, p, zl * 64 : zl * 64 + 64] = sorted_rows[p * 64 : p * 64 + 64]
        parts = half_silu(0.5 * nt_dot(cand_v[...].reshape(768, 1024), W[keep, hi].reshape(512, 1024))).astype(BF16)
        own_keys, own_values = parts[:, :128], parts[:, 128:256]
        queries, user_gate = parts[:, 256:384], parts[:, 384:]
        own = jnp.dot(queries * own_keys, jnp.ones((128, 128), BF16), preferred_element_type=F32)
        own = half_silu(own * score_half) * own_values.astype(F32)
        for user in range(users_here):
            rows_u = slice(user * 384, user * 384 + 384)
            Q[keep, hi, user] = queries[rows_u]
            gate[user, :, at] = user_gate[rows_u]
            attn[user, :, at] = own[rows_u]

    def keys_values(t, hi):
        w_kv = W[lax.rem(t, 2), hi, 0:2].reshape(256, 1024)
        kv = half_silu(0.5 * nt_dot(H[...].reshape(512, 1024), w_kv))
        KV[t, hi, c, :, :128] = kv[:, :128].astype(BF16)
        KV[t, hi, c, :, 128:] = (kv[:, 128:] * mask_v[...]).astype(BF16)
        kv_copy(t, hi, c).start()

    def attend(t, hi, user):
        keep, at = lax.rem(t, 2), columns_of(t, hi)
        keys, values = KV[t, hi, user, :, :128], KV[t, hi, user, :, 128:]
        weights = half_silu(nt_dot(Q[keep, hi, user], keys) * score_half).astype(BF16)
        attn[user, :, at] += jnp.dot(weights, values, preferred_element_type=F32)

    def both(work, t):
        for hi in range(2):
            work(t, hi)

    def chunk(t, carry):
        @pl.when(t == 1)
        def _():
            settle(hist_plan[1])

        @pl.when(t > 0)
        def _():
            both(keys_values, t - 1)
            both(functools.partial(attend, user=c), t - 1)
            for hi in range(2):
                kv_copy(t - 1, hi, oc).wait_recv()
            both(functools.partial(attend, user=oc), t - 1)

        for w in (2, 3, 4):
            @pl.when(t == w - 1)
            def _():
                twin_wait(w)

        @pl.when(t < 4)
        def _():
            both(project, t)

        def forward(w):
            ring_wait(w)
            if w < 4:
                ring_send(w + 1)
            if w < 4:
                settle(later[w - 1])
            twin_send(w)

        for w in (2, 3, 4):
            @pl.when(t == w - 2)
            def _():
                forward(w)

        return carry

    def kv_copy(t, hi, whose):
        k = kv_sems[0] + t * 2 + hi
        return pltpu.make_async_remote_copy(
            src_ref=KV.at[t, hi, whose], dst_ref=KV.at[t, hi, whose],
            send_sem=send_sem.at[k], recv_sem=recv_sem.at[k], device_id=sib, device_id_type=MESH,
        )

    lax.fori_loop(0, HEADS // 2 + 1, chunk, 0)

    slot0 = s * 384

    def norm(user, block):
        rows_a = attn[user, block]
        mean = jnp.sum(rows_a, axis=1, keepdims=True) * (1.0 / 1024)
        centered = rows_a - mean
        var = jnp.sum(centered * centered, axis=1, keepdims=True) * (1.0 / 1024)
        normed = centered * lax.rsqrt(var + 1e-06)
        gated[user, block] = (normed * gate[user, block].astype(F32)).astype(BF16)

    def norm_step(i, carry):
        norm(0, pl.ds(pl.multiple_of(i * 64, 64), 64))
        return carry

    lax.fori_loop(0, 6, norm_step, 0)
    for user in range(users_here):
        for n in range(4):
            ncols = pl.ds(n * 256, 256)
            mixed = jnp.dot(gated[user], ow_v[:, ncols], preferred_element_type=F32)
            mixed = mixed + cand_v[user, :, ncols].astype(F32)
            slot = slot0 + lax.broadcasted_iota(jnp.int32, (384, 256), 0)
            out_v[user, :, ncols] = jnp.where(slot < ccount_ref[user], mixed, 0.0).astype(BF16)
            if user == 0:
                for piece in range(3):
                    norm(1, pl.ds(n * 96 + piece * 32, 32))
        pltpu.make_async_copy(out_v.at[user], out_ref.at[user], local_sem.at[3 + user]).start()
    for user in range(users_here):
        pltpu.make_async_copy(out_v.at[user], out_ref.at[user], local_sem.at[3 + user]).wait()
    for number in range(HEADS):
        kv_copy(number // 2, number % 2, c).wait_send()
    for src, k in sent:
        rcopy(src, src, k, sib).wait_send()
    assert state["k"] <= NSEM


def body(candidates, history, proj_weight, out_weight, hist_len, cand_count):
    anyspace = pl.BlockSpec(memory_space=pl.ANY)
    smem = pl.BlockSpec(memory_space=pltpu.SMEM)
    vmem = pl.BlockSpec(memory_space=pltpu.VMEM)
    return pl.pallas_call(
        kernel,
        out_shape=jax.ShapeDtypeStruct(candidates.shape, BF16),
        in_specs=[anyspace, anyspace, vmem, anyspace, smem, smem],
        out_specs=anyspace,
        scratch_shapes=[
            pltpu.VMEM((2, NX, NY, NZ, 16, 1024), BF16),
            pltpu.VMEM((NX, 2, 2, 32, 1024), BF16),
            pltpu.VMEM((4, 2, 2, 512, 256), BF16),
            pltpu.VMEM((2, 2, 2, 384, 128), BF16),
            pltpu.VMEM((2, 2, 4, 128, 1024), BF16),
            pltpu.VMEM((256, 256), BF16),
            pltpu.VMEM((2, 384, 1024), BF16),
            pltpu.VMEM((1024, 1024), BF16),
            pltpu.VMEM((512, 128), F32),
            pltpu.VMEM((2, 384, 1024), F32),
            pltpu.VMEM((2, 384, 1024), BF16),
            pltpu.VMEM((2, 384, 1024), BF16),
            pltpu.VMEM((2, 384, 1024), BF16),
            pltpu.SemaphoreType.DMA((NSEM,)),
            pltpu.SemaphoreType.DMA((NSEM,)),
            pltpu.SemaphoreType.DMA((5,)),
        ],
        compiler_params=pltpu.CompilerParams(
            collective_id=0, has_side_effects=True, vmem_limit_bytes=56 * 1024 * 1024
        ),
    )(candidates, history, proj_weight, out_weight, hist_len, cand_count)


def solution(mesh):
    in_specs = (
        P("users", "score", None),
        P("users", "score", None),
        P(("users", "score"), None, None),
        P(),
        P("users"),
        P("users"),
    )
    out_specs = P("users", "score", None)
    return jax.shard_map(body, mesh=mesh, in_specs=in_specs, out_specs=out_specs, check_vma=False)
```

```python
import functools
import math

import jax
import jax.numpy as jnp
from jax import lax
from jax.experimental import pallas as pl
from jax.experimental.pallas import tpu as pltpu
from jax.sharding import PartitionSpec as P

MESH = pl.DeviceIdType.MESH
HEADS = 8
NX, NY, NZ = 4, 4, 8
BF16, F32 = jnp.bfloat16, jnp.float32
COLS_X, COLS_Y, COLS_Z = pl.ds(0, 256), pl.ds(256, 384), pl.ds(640, 384)
COLS_XY = pl.ds(0, 640)
SLOT = {0: 0, -1: 1, 1: 2, -2: 3, 2: 4, -3: 5, 3: 6, 4: 7, -4: 7}
NSEM = 128


def nt_dot(a, b):
    return lax.dot_general(a, b, (((1,), (1,)), ((), ())), preferred_element_type=F32)


def half_silu(t):
    return t + t * jnp.tanh(t)


def kernel(
    cand_ref, hist_ref, proj_ref, ow_ref, hlen_ref, ccount_ref, out_ref,
    G, H, KV, Q, W, pick_v, cand_v, ow_v, mask_v, attn, gate, gated, out_v, send_sem, recv_sem, local_sem,
):
    u = lax.axis_index("users")
    s = lax.axis_index("score")
    z = lax.rem(u, NZ)
    yhi = lax.div(u, NZ)
    c = lax.rem(s, 2)
    x = lax.rem(lax.div(s, 2), NX)
    ylo = lax.div(s, 8)
    y = yhi * 2 + ylo
    oc = 1 - c

    def dev(px, py, pz, pc):
        return (lax.div(py, 2) * NZ + pz, lax.rem(py, 2) * 8 + px * 2 + pc)

    def up(pos, n, k):
        return lax.rem(pos + k + n, n)

    yo = y + 1 - 2 * ylo
    sib = dev(x, y, z, oc)
    local = [
        pltpu.make_async_copy(hist_ref.at[c], H.at[x, ylo, c], local_sem.at[0]),
        pltpu.make_async_copy(cand_ref, cand_v, local_sem.at[1]),
        pltpu.make_async_copy(ow_ref, ow_v, local_sem.at[2]),
    ]
    for copy in local:
        copy.start()

    barrier = pltpu.get_barrier_semaphore()
    partners = [dev(up(x, NX, k), y, z, c) for k in (1, 3, 2)] + [dev(x, up(y, NY, k), z, c) for k in (1, 3, 2)]
    partners += [dev(x, y, up(z, NZ, k), c) for k in (1, 7, 2, 6, 3, 5, 4)] + [sib, dev(x, yo, z, oc)]
    for partner in partners:
        pl.semaphore_signal(barrier, inc=1, device_id=partner, device_id_type=MESH)

    row16 = lax.broadcasted_iota(jnp.int32, (16, 1024), 0)
    tile = jnp.zeros((16, 1024), F32)
    for f in range(4):
        rows_f = proj_ref[f].astype(F32)
        for p in range(4):
            tile = jnp.where(row16 == f * 4 + p, jnp.broadcast_to(rows_f[p : p + 1], (16, 1024)), tile)
    G[c, x, y, 0] = tile.astype(BF16)

    pl.semaphore_wait(barrier, len(partners))

    state = {"k": 0}
    sent = []

    def new_sem():
        k = state["k"]
        state["k"] = k + 1
        return k

    def rcopy(src, dst, k, target):
        return pltpu.make_async_remote_copy(
            src_ref=src(), dst_ref=dst(), send_sem=send_sem.at[k], recv_sem=recv_sem.at[k],
            device_id=target, device_id_type=MESH,
        )

    def send(src, dst, k, target):
        rcopy(src, dst, k, target).start()
        sent.append((src, k))

    def wait(dst, k):
        rcopy(dst, dst, k, sib).wait_recv()

    hist_arrivals = []
    for who, target, py, pc in (
        (oc, sib, ylo, oc), (c, dev(x, yo, z, c), 1 - ylo, c), (oc, dev(x, yo, z, oc), 1 - ylo, oc),
    ):
        k = new_sem()
        send(functools.partial(hist_ref.at.__getitem__, who), lambda: H.at[x, ylo, c], k, target)
        hist_arrivals.append((functools.partial(H.at.__getitem__, (x, py, pc)), k))

    whole = slice(None)

    def view(plane, xs, ys, slots, columns):
        return lambda: G.at[plane, xs, ys, slots, :, columns]

    def direct(axis, block):
        n, at = (NX, x) if axis == "x" else (NY, y)
        arrivals = []
        for step in (1, 3, 2):
            k = new_sem()
            to = up(at, n, step)
            send(block(at), block(at), k, dev(to, y, z, c) if axis == "x" else dev(x, to, z, c))
            arrivals.append((block(up(at, n, -step)), k))
        return arrivals

    def settle(arrivals):
        for where, k in arrivals:
            wait(where, k)

    waves = {2: pl.ds(3, 2), 3: pl.ds(5, 2), 4: pl.ds(7, 1)}
    groups = [pl.ds(0, 3), pl.ds(3, 2), pl.ds(5, 3)]

    def second(w):
        group_x = direct("y", lambda at: view(c, x, at, groups[w], COLS_X))
        group_y = direct("x", lambda at: view(c, at, y, groups[w], COLS_Y))
        return group_x, group_y

    def third(w, arrivals):
        settle(arrivals[0])
        group_x = direct("x", lambda at: view(c, at, whole, groups[w], COLS_X))
        settle(arrivals[1])
        group_y = direct("y", lambda at: view(c, whole, at, groups[w], COLS_Y))
        return group_x + group_y

    along_z = {}

    def z_send(off):
        k = new_sem()
        send(view(c, x, y, 0, COLS_XY), view(c, x, y, SLOT[-off], COLS_XY), k, dev(x, y, up(z, NZ, off), c))
        along_z[SLOT[-off]] = (view(c, x, y, SLOT[-off], COLS_XY), k)

    zx = direct("x", lambda at: view(c, at, y, 0, COLS_Z))
    for off in (1, -1, 2, -2, 3, -3, 4):
        z_send(off)
    settle([along_z[1], along_z[2]])
    stage2 = {0: second(0)}
    settle(zx)
    zy = direct("y", lambda at: view(c, whole, at, 0, COLS_Z))
    settle([along_z[3], along_z[4]])
    stage2[1] = second(1)
    settle(zy)

    z_right, z_left = dev(x, y, up(z, NZ, 1), c), dev(x, y, up(z, NZ, -1), c)
    ring_sems = [(new_sem(), new_sem()) for _ in range(4)]
    first_xy, first_z = new_sem(), new_sem()
    twin_sems = {w: new_sem() for w in (2, 3, 4)}
    kv_sems = [new_sem() for _ in range(HEADS)]

    def ring_blocks(w):
        xs = (whole, whole) if w < 4 else (pl.ds(0, 2), pl.ds(2, 2))
        down, high = (2 * w - 3, 2 * w - 2) if w > 1 else (0, 0)
        into = (2 * w - 1, 2 * w) if w < 4 else (7, 7)
        return [
            (view(c, xs[0], whole, down, COLS_Z), view(c, xs[0], whole, into[0], COLS_Z)),
            (view(c, xs[1], whole, high, COLS_Z), view(c, xs[1], whole, into[1], COLS_Z)),
        ]

    def ring_send(w):
        for (src, dst), k, target in zip(ring_blocks(w), ring_sems[w - 1], (z_right, z_left)):
            send(src, dst, k, target)

    def ring_wait(w):
        for (_, dst), k in zip(ring_blocks(w), ring_sems[w - 1]):
            wait(dst, k)

    def twin_send(w):
        block = view(c, whole, whole, waves[w], whole)
        send(block, block, twin_sems[w], sib)

    def twin_wait(w):
        wait(view(oc, whole, whole, waves[w], whole), twin_sems[w])

    ring_send(1)
    stage3 = third(0, stage2[0])
    local[0].wait()
    settle(hist_arrivals)
    hist_x = direct("x", lambda at: lambda: H.at[at])
    settle([along_z[5], along_z[6], along_z[7]])
    stage2[2] = second(2)
    ring_wait(1)
    ring_send(2)
    block = view(c, whole, whole, groups[0], COLS_Z)
    send(block, block, first_z, sib)
    later = {1: third(1, stage2[1])}
    settle(stage3)
    block_xy = view(c, whole, whole, groups[0], COLS_XY)
    send(block_xy, block_xy, first_xy, sib)
    local[1].wait()
    local[2].wait()
    wait(view(oc, whole, whole, groups[0], COLS_Z), first_z)
    wait(view(oc, whole, whole, groups[0], COLS_XY), first_xy)
    later[2] = third(2, stage2[2])

    head_size = 128
    score_half = 0.5 / math.sqrt(head_size)
    users_here = cand_v.shape[0]

    q = lax.broadcasted_iota(jnp.int32, (512, 128), 0)
    event = (((q >> 6) & 1) * 8 + (q >> 7) * 2 + ((q >> 5) & 1)) * 32 + (q & 31)
    mask_v[...] = (event < hlen_ref[c]).astype(F32)
    out_row = lax.broadcasted_iota(jnp.int32, (256, 256), 0)
    in_row = lax.broadcasted_iota(jnp.int32, (256, 256), 1)
    source = ((out_row & 63) >> 2) * 16 + (out_row & 3) * 4 + (out_row >> 6)
    pick_v[...] = (in_row == source).astype(F32).astype(BF16)

    odd = lax.rem(z, 2)

    def slabs(hi, slot):
        return jnp.concatenate(
            [G[plane, px, hi * 2 + yl, slot] for yl in range(2) for px in range(NX) for plane in range(2)],
            axis=0,
        )

    def choose(t, even_slots, odd_slots):
        slot = jnp.int32(0)
        for number in range(4):
            slot = jnp.where(t == number, jnp.where(odd == 1, odd_slots[number], even_slots[number]), slot)
        return slot

    def pair_of(t):
        turn = t + lax.div(t, 2) - 2 * lax.div(t, 3)
        return lax.rem(lax.div(z, 2) + (2 * odd - 1) * turn + 8, 4)

    def columns_of(t, hi):
        return pl.ds(pl.multiple_of((hi * 4 + pair_of(t)) * 128, 128), 128)

    def project(t, hi):
        slots = (choose(t, (0, 3, 4, 7), (1, 2, 5, 6)), choose(t, (2, 1, 6, 5), (0, 4, 3, 7)))
        keep, at = lax.rem(t, 2), columns_of(t, hi)
        for zl in range(2):
            sorted_rows = jnp.dot(pick_v[...], slabs(hi, slots[zl]), preferred_element_type=F32).astype(BF16)
            for p in range(4):
                W[keep, hi, p, zl * 64 : zl * 64 + 64] = sorted_rows[p * 64 : p * 64 + 64]
        parts = half_silu(0.5 * nt_dot(cand_v[...].reshape(768, 1024), W[keep, hi].reshape(512, 1024))).astype(BF16)
        own_keys, own_values = parts[:, :128], parts[:, 128:256]
        queries, user_gate = parts[:, 256:384], parts[:, 384:]
        own = jnp.dot(queries * own_keys, jnp.ones((128, 128), BF16), preferred_element_type=F32)
        own = half_silu(own * score_half) * own_values.astype(F32)
        for user in range(users_here):
            rows_u = slice(user * 384, user * 384 + 384)
            Q[keep, hi, user] = queries[rows_u]
            gate[user, :, at] = user_gate[rows_u]
            attn[user, :, at] = own[rows_u]

    def keys_values(t, hi):
        w_kv = W[lax.rem(t, 2), hi, 0:2].reshape(256, 1024)
        kv = half_silu(0.5 * nt_dot(H[...].reshape(512, 1024), w_kv))
        KV[t, hi, c, :, :128] = kv[:, :128].astype(BF16)
        KV[t, hi, c, :, 128:] = (kv[:, 128:] * mask_v[...]).astype(BF16)
        kv_copy(t, hi, c).start()

    def attend(t, hi, user):
        keep, at = lax.rem(t, 2), columns_of(t, hi)
        keys, values = KV[t, hi, user, :, :128], KV[t, hi, user, :, 128:]
        weights = half_silu(nt_dot(Q[keep, hi, user], keys) * score_half).astype(BF16)
        attn[user, :, at] += jnp.dot(weights, values, preferred_element_type=F32)

    def both(work, t):
        for hi in range(2):
            work(t, hi)

    def chunk(t, carry):
        @pl.when(t == 1)
        def _():
            settle(hist_x)

        @pl.when(t > 0)
        def _():
            both(keys_values, t - 1)
            both(functools.partial(attend, user=c), t - 1)
            for hi in range(2):
                kv_copy(t - 1, hi, oc).wait_recv()
            both(functools.partial(attend, user=oc), t - 1)

        for w in (2, 3, 4):
            @pl.when(t == w - 1)
            def _():
                twin_wait(w)

        @pl.when(t < 4)
        def _():
            both(project, t)

        def forward(w):
            ring_wait(w)
            if w < 4:
                ring_send(w + 1)
            if w < 4:
                settle(later[w - 1])
            twin_send(w)

        for w in (2, 3, 4):
            @pl.when(t == w - 2)
            def _():
                forward(w)

        return carry

    def kv_copy(t, hi, whose):
        k = kv_sems[0] + t * 2 + hi
        return pltpu.make_async_remote_copy(
            src_ref=KV.at[t, hi, whose], dst_ref=KV.at[t, hi, whose],
            send_sem=send_sem.at[k], recv_sem=recv_sem.at[k], device_id=sib, device_id_type=MESH,
        )

    lax.fori_loop(0, HEADS // 2 + 1, chunk, 0)

    slot0 = s * 384

    def norm(user, block):
        rows_a = attn[user, block]
        mean = jnp.sum(rows_a, axis=1, keepdims=True) * (1.0 / 1024)
        centered = rows_a - mean
        var = jnp.sum(centered * centered, axis=1, keepdims=True) * (1.0 / 1024)
        normed = centered * lax.rsqrt(var + 1e-06)
        gated[user, block] = (normed * gate[user, block].astype(F32)).astype(BF16)

    def norm_step(i, carry):
        norm(0, pl.ds(pl.multiple_of(i * 64, 64), 64))
        return carry

    lax.fori_loop(0, 6, norm_step, 0)
    for user in range(users_here):
        for n in range(4):
            ncols = pl.ds(n * 256, 256)
            mixed = jnp.dot(gated[user], ow_v[:, ncols], preferred_element_type=F32)
            mixed = mixed + cand_v[user, :, ncols].astype(F32)
            slot = slot0 + lax.broadcasted_iota(jnp.int32, (384, 256), 0)
            out_v[user, :, ncols] = jnp.where(slot < ccount_ref[user], mixed, 0.0).astype(BF16)
            if user == 0:
                for piece in range(3):
                    norm(1, pl.ds(n * 96 + piece * 32, 32))
        pltpu.make_async_copy(out_v.at[user], out_ref.at[user], local_sem.at[3 + user]).start()
    for user in range(users_here):
        pltpu.make_async_copy(out_v.at[user], out_ref.at[user], local_sem.at[3 + user]).wait()
    for number in range(HEADS):
        kv_copy(number // 2, number % 2, c).wait_send()
    for src, k in sent:
        rcopy(src, src, k, sib).wait_send()
    assert state["k"] <= NSEM


def body(candidates, history, proj_weight, out_weight, hist_len, cand_count):
    anyspace = pl.BlockSpec(memory_space=pl.ANY)
    smem = pl.BlockSpec(memory_space=pltpu.SMEM)
    vmem = pl.BlockSpec(memory_space=pltpu.VMEM)
    return pl.pallas_call(
        kernel,
        out_shape=jax.ShapeDtypeStruct(candidates.shape, BF16),
        in_specs=[anyspace, anyspace, vmem, anyspace, smem, smem],
        out_specs=anyspace,
        scratch_shapes=[
            pltpu.VMEM((2, NX, NY, NZ, 16, 1024), BF16),
            pltpu.VMEM((NX, 2, 2, 32, 1024), BF16),
            pltpu.VMEM((4, 2, 2, 512, 256), BF16),
            pltpu.VMEM((2, 2, 2, 384, 128), BF16),
            pltpu.VMEM((2, 2, 4, 128, 1024), BF16),
            pltpu.VMEM((256, 256), BF16),
            pltpu.VMEM((2, 384, 1024), BF16),
            pltpu.VMEM((1024, 1024), BF16),
            pltpu.VMEM((512, 128), F32),
            pltpu.VMEM((2, 384, 1024), F32),
            pltpu.VMEM((2, 384, 1024), BF16),
            pltpu.VMEM((2, 384, 1024), BF16),
            pltpu.VMEM((2, 384, 1024), BF16),
            pltpu.SemaphoreType.DMA((NSEM,)),
            pltpu.SemaphoreType.DMA((NSEM,)),
            pltpu.SemaphoreType.DMA((5,)),
        ],
        compiler_params=pltpu.CompilerParams(
            collective_id=0, has_side_effects=True, vmem_limit_bytes=56 * 1024 * 1024
        ),
    )(candidates, history, proj_weight, out_weight, hist_len, cand_count)


def solution(mesh):
    in_specs = (
        P("users", "score", None),
        P("users", "score", None),
        P(("users", "score"), None, None),
        P(),
        P("users"),
        P("users"),
    )
    out_specs = P("users", "score", None)
    return jax.shard_map(body, mesh=mesh, in_specs=in_specs, out_specs=out_specs, check_vma=False)
```

```python
import functools
import math

import jax
import jax.numpy as jnp
from jax import lax
from jax.experimental import pallas as pl
from jax.experimental.pallas import tpu as pltpu
from jax.sharding import PartitionSpec as P

MESH = pl.DeviceIdType.MESH
HEADS = 8
NX, NY, NZ = 4, 4, 8
BF16, F32 = jnp.bfloat16, jnp.float32
COLS_X, COLS_Y, COLS_Z = pl.ds(0, 256), pl.ds(256, 384), pl.ds(640, 384)
COLS_XY = pl.ds(0, 640)
SLOT = {0: 0, -1: 1, 1: 2, -2: 3, 2: 4, -3: 5, 3: 6, 4: 7, -4: 7}
NSEM = 128


def nt_dot(a, b):
    return lax.dot_general(a, b, (((1,), (1,)), ((), ())), preferred_element_type=F32)


def half_silu(t):
    return t + t * jnp.tanh(t)


def kernel(
    cand_ref, hist_ref, proj_ref, ow_ref, hlen_ref, ccount_ref, out_ref,
    G, H, KV, Q, W, pick_v, cand_v, ow_v, mask_v, attn, gate, gated, out_v, send_sem, recv_sem, local_sem,
):
    u = lax.axis_index("users")
    s = lax.axis_index("score")
    z = lax.rem(u, NZ)
    yhi = lax.div(u, NZ)
    c = lax.rem(s, 2)
    x = lax.rem(lax.div(s, 2), NX)
    ylo = lax.div(s, 8)
    y = yhi * 2 + ylo
    oc = 1 - c

    def dev(px, py, pz, pc):
        return (lax.div(py, 2) * NZ + pz, lax.rem(py, 2) * 8 + px * 2 + pc)

    def up(pos, n, k):
        return lax.rem(pos + k + n, n)

    yo = y + 1 - 2 * ylo
    sib = dev(x, y, z, oc)
    local = [
        pltpu.make_async_copy(hist_ref.at[c], H.at[x, ylo, c], local_sem.at[0]),
        pltpu.make_async_copy(cand_ref, cand_v, local_sem.at[1]),
        pltpu.make_async_copy(ow_ref, ow_v, local_sem.at[2]),
    ]
    for copy in local:
        copy.start()

    barrier = pltpu.get_barrier_semaphore()
    partners = [dev(up(x, NX, k), y, z, c) for k in (1, 3, 2)] + [dev(x, up(y, NY, k), z, c) for k in (1, 3, 2)]
    partners += [dev(x, y, up(z, NZ, k), c) for k in (1, 7, 2, 6, 3, 5, 4)] + [sib, dev(x, yo, z, oc)]
    for partner in partners:
        pl.semaphore_signal(barrier, inc=1, device_id=partner, device_id_type=MESH)

    row16 = lax.broadcasted_iota(jnp.int32, (16, 1024), 0)
    tile = jnp.zeros((16, 1024), F32)
    for f in range(4):
        rows_f = proj_ref[f].astype(F32)
        for p in range(4):
            tile = jnp.where(row16 == f * 4 + p, jnp.broadcast_to(rows_f[p : p + 1], (16, 1024)), tile)
    G[c, x, y, 0] = tile.astype(BF16)

    pl.semaphore_wait(barrier, len(partners))

    state = {"k": 0}
    sent = []

    def new_sem():
        k = state["k"]
        state["k"] = k + 1
        return k

    def rcopy(src, dst, k, target):
        return pltpu.make_async_remote_copy(
            src_ref=src(), dst_ref=dst(), send_sem=send_sem.at[k], recv_sem=recv_sem.at[k],
            device_id=target, device_id_type=MESH,
        )

    def send(src, dst, k, target):
        rcopy(src, dst, k, target).start()
        sent.append((src, k))

    def wait(dst, k):
        rcopy(dst, dst, k, sib).wait_recv()

    hist_arrivals = []
    for who, target, py, pc in (
        (oc, sib, ylo, oc), (c, dev(x, yo, z, c), 1 - ylo, c), (oc, dev(x, yo, z, oc), 1 - ylo, oc),
    ):
        k = new_sem()
        send(functools.partial(hist_ref.at.__getitem__, who), lambda: H.at[x, ylo, c], k, target)
        hist_arrivals.append((functools.partial(H.at.__getitem__, (x, py, pc)), k))

    whole = slice(None)

    def view(plane, xs, ys, slots, columns):
        return lambda: G.at[plane, xs, ys, slots, :, columns]

    def direct(axis, block):
        n, at = (NX, x) if axis == "x" else (NY, y)
        arrivals = []
        for step in (1, 3, 2):
            k = new_sem()
            to = up(at, n, step)
            send(block(at), block(at), k, dev(to, y, z, c) if axis == "x" else dev(x, to, z, c))
            arrivals.append((block(up(at, n, -step)), k))
        return arrivals

    def settle(arrivals):
        for where, k in arrivals:
            wait(where, k)

    waves = {2: pl.ds(3, 2), 3: pl.ds(5, 2), 4: pl.ds(7, 1)}
    groups = [pl.ds(0, 3), pl.ds(3, 2), pl.ds(5, 3)]

    def second(w):
        group_x = direct("y", lambda at: view(c, x, at, groups[w], COLS_X))
        group_y = direct("x", lambda at: view(c, at, y, groups[w], COLS_Y))
        return group_x, group_y

    def third(w, arrivals):
        settle(arrivals[0])
        group_x = direct("x", lambda at: view(c, at, whole, groups[w], COLS_X))
        settle(arrivals[1])
        group_y = direct("y", lambda at: view(c, whole, at, groups[w], COLS_Y))
        return group_x + group_y

    spot = {"x": [up(x, NX, k) for k in range(NX)], "y": [up(y, NY, k) for k in range(NY)]}
    neighbour = {
        "x": [dev(spot["x"][k], y, z, c) for k in range(NX)],
        "y": [dev(x, spot["y"][k], z, c) for k in range(NY)],
    }

    def ring_plan(axis, block):
        first = [(block(spot[axis][3], None), new_sem()), (block(spot[axis][1], None), new_sem())]
        return first, [(block(spot[axis][2], half), new_sem()) for half in range(2)]

    def ring_first(axis, block, plan):
        for (_, k), step in zip(plan[0], (1, 3)):
            send(block(spot[axis][0], None), block(spot[axis][0], None), k, neighbour[axis][step])

    def ring_second(axis, block, plan):
        settle(plan[0])
        for half, step in ((0, 1), (1, 3)):
            mine = block(spot[axis][4 - step], half)
            send(mine, mine, plan[1][half][1], neighbour[axis][step])

    def hist_block(at, half):
        return (lambda: H.at[at]) if half is None else (lambda: H.at[at, half])

    hist_plan = ring_plan("x", hist_block)
    along_z = {}

    def z_send(off):
        k = new_sem()
        send(view(c, x, y, 0, COLS_XY), view(c, x, y, SLOT[-off], COLS_XY), k, dev(x, y, up(z, NZ, off), c))
        along_z[SLOT[-off]] = (view(c, x, y, SLOT[-off], COLS_XY), k)

    zx = direct("x", lambda at: view(c, at, y, 0, COLS_Z))
    for off in (1, -1, 2, -2, 3, -3, 4):
        z_send(off)
    settle([along_z[1], along_z[2]])
    stage2 = {0: second(0)}
    local[0].wait()
    settle(hist_arrivals)
    ring_first("x", hist_block, hist_plan)
    settle(zx)
    zy = direct("y", lambda at: view(c, whole, at, 0, COLS_Z))
    settle([along_z[3], along_z[4]])
    stage2[1] = second(1)
    settle(zy)

    z_right, z_left = dev(x, y, up(z, NZ, 1), c), dev(x, y, up(z, NZ, -1), c)
    ring_sems = [(new_sem(), new_sem()) for _ in range(4)]
    first_xy, first_z = new_sem(), new_sem()
    twin_sems = {w: new_sem() for w in (2, 3, 4)}
    kv_sems = [new_sem() for _ in range(HEADS)]

    def ring_blocks(w):
        xs = (whole, whole) if w < 4 else (pl.ds(0, 2), pl.ds(2, 2))
        down, high = (2 * w - 3, 2 * w - 2) if w > 1 else (0, 0)
        into = (2 * w - 1, 2 * w) if w < 4 else (7, 7)
        return [
            (view(c, xs[0], whole, down, COLS_Z), view(c, xs[0], whole, into[0], COLS_Z)),
            (view(c, xs[1], whole, high, COLS_Z), view(c, xs[1], whole, into[1], COLS_Z)),
        ]

    def ring_send(w):
        for (src, dst), k, target in zip(ring_blocks(w), ring_sems[w - 1], (z_right, z_left)):
            send(src, dst, k, target)

    def ring_wait(w):
        for (_, dst), k in zip(ring_blocks(w), ring_sems[w - 1]):
            wait(dst, k)

    def twin_send(w):
        block = view(c, whole, whole, waves[w], whole)
        send(block, block, twin_sems[w], sib)

    def twin_wait(w):
        wait(view(oc, whole, whole, waves[w], whole), twin_sems[w])

    ring_send(1)
    stage3 = third(0, stage2[0])
    settle([along_z[5], along_z[6], along_z[7]])
    stage2[2] = second(2)
    ring_wait(1)
    ring_send(2)
    block = view(c, whole, whole, groups[0], COLS_Z)
    send(block, block, first_z, sib)
    later = {1: third(1, stage2[1])}
    settle(stage3)
    block_xy = view(c, whole, whole, groups[0], COLS_XY)
    send(block_xy, block_xy, first_xy, sib)
    ring_second("x", hist_block, hist_plan)
    later[2] = third(2, stage2[2])
    local[1].wait()
    local[2].wait()
    wait(view(oc, whole, whole, groups[0], COLS_Z), first_z)
    wait(view(oc, whole, whole, groups[0], COLS_XY), first_xy)

    head_size = 128
    score_half = 0.5 / math.sqrt(head_size)
    users_here = cand_v.shape[0]

    q = lax.broadcasted_iota(jnp.int32, (512, 128), 0)
    event = (((q >> 6) & 1) * 8 + (q >> 7) * 2 + ((q >> 5) & 1)) * 32 + (q & 31)
    mask_v[...] = (event < hlen_ref[c]).astype(F32)
    out_row = lax.broadcasted_iota(jnp.int32, (256, 256), 0)
    in_row = lax.broadcasted_iota(jnp.int32, (256, 256), 1)
    source = ((out_row & 63) >> 2) * 16 + (out_row & 3) * 4 + (out_row >> 6)
    pick_v[...] = (in_row == source).astype(F32).astype(BF16)

    odd = lax.rem(z, 2)

    def slabs(hi, slot):
        return jnp.concatenate(
            [G[plane, px, hi * 2 + yl, slot] for yl in range(2) for px in range(NX) for plane in range(2)],
            axis=0,
        )

    def choose(t, even_slots, odd_slots):
        slot = jnp.int32(0)
        for number in range(4):
            slot = jnp.where(t == number, jnp.where(odd == 1, odd_slots[number], even_slots[number]), slot)
        return slot

    def pair_of(t):
        turn = t + lax.div(t, 2) - 2 * lax.div(t, 3)
        return lax.rem(lax.div(z, 2) + (2 * odd - 1) * turn + 8, 4)

    def columns_of(t, hi):
        return pl.ds(pl.multiple_of((hi * 4 + pair_of(t)) * 128, 128), 128)

    def project(t, hi):
        slots = (choose(t, (0, 3, 4, 7), (1, 2, 5, 6)), choose(t, (2, 1, 6, 5), (0, 4, 3, 7)))
        keep, at = lax.rem(t, 2), columns_of(t, hi)
        for zl in range(2):
            sorted_rows = jnp.dot(pick_v[...], slabs(hi, slots[zl]), preferred_element_type=F32).astype(BF16)
            for p in range(4):
                W[keep, hi, p, zl * 64 : zl * 64 + 64] = sorted_rows[p * 64 : p * 64 + 64]
        parts = half_silu(0.5 * nt_dot(cand_v[...].reshape(768, 1024), W[keep, hi].reshape(512, 1024))).astype(BF16)
        own_keys, own_values = parts[:, :128], parts[:, 128:256]
        queries, user_gate = parts[:, 256:384], parts[:, 384:]
        own = jnp.dot(queries * own_keys, jnp.ones((128, 128), BF16), preferred_element_type=F32)
        own = half_silu(own * score_half) * own_values.astype(F32)
        for user in range(users_here):
            rows_u = slice(user * 384, user * 384 + 384)
            Q[keep, hi, user] = queries[rows_u]
            gate[user, :, at] = user_gate[rows_u]
            attn[user, :, at] = own[rows_u]

    def keys_values(t, hi):
        w_kv = W[lax.rem(t, 2), hi, 0:2].reshape(256, 1024)
        kv = half_silu(0.5 * nt_dot(H[...].reshape(512, 1024), w_kv))
        KV[t, hi, c, :, :128] = kv[:, :128].astype(BF16)
        KV[t, hi, c, :, 128:] = (kv[:, 128:] * mask_v[...]).astype(BF16)
        kv_copy(t, hi, c).start()

    def attend(t, hi, user):
        keep, at = lax.rem(t, 2), columns_of(t, hi)
        keys, values = KV[t, hi, user, :, :128], KV[t, hi, user, :, 128:]
        weights = half_silu(nt_dot(Q[keep, hi, user], keys) * score_half).astype(BF16)
        attn[user, :, at] += jnp.dot(weights, values, preferred_element_type=F32)

    def both(work, t):
        for hi in range(2):
            work(t, hi)

    def chunk(t, carry):
        @pl.when(t == 1)
        def _():
            settle(hist_plan[1])

        @pl.when(t > 0)
        def _():
            both(keys_values, t - 1)
            both(functools.partial(attend, user=c), t - 1)
            for hi in range(2):
                kv_copy(t - 1, hi, oc).wait_recv()
            both(functools.partial(attend, user=oc), t - 1)

        for w in (2, 3, 4):
            @pl.when(t == w - 1)
            def _():
                twin_wait(w)

        @pl.when(t < 4)
        def _():
            both(project, t)

        def forward(w):
            ring_wait(w)
            if w < 4:
                ring_send(w + 1)
            if w < 4:
                settle(later[w - 1])
            twin_send(w)

        for w in (2, 3, 4):
            @pl.when(t == w - 2)
            def _():
                forward(w)

        return carry

    def kv_copy(t, hi, whose):
        k = kv_sems[0] + t * 2 + hi
        return pltpu.make_async_remote_copy(
            src_ref=KV.at[t, hi, whose], dst_ref=KV.at[t, hi, whose],
            send_sem=send_sem.at[k], recv_sem=recv_sem.at[k], device_id=sib, device_id_type=MESH,
        )

    lax.fori_loop(0, HEADS // 2 + 1, chunk, 0)

    slot0 = s * 384

    def norm(user, block):
        rows_a = attn[user, block]
        mean = jnp.sum(rows_a, axis=1, keepdims=True) * (1.0 / 1024)
        centered = rows_a - mean
        var = jnp.sum(centered * centered, axis=1, keepdims=True) * (1.0 / 1024)
        normed = centered * lax.rsqrt(var + 1e-06)
        gated[user, block] = (normed * gate[user, block].astype(F32)).astype(BF16)

    def norm_step(i, carry):
        norm(0, pl.ds(pl.multiple_of(i * 64, 64), 64))
        return carry

    lax.fori_loop(0, 6, norm_step, 0)
    for user in range(users_here):
        for n in range(4):
            ncols = pl.ds(n * 256, 256)
            mixed = jnp.dot(gated[user], ow_v[:, ncols], preferred_element_type=F32)
            mixed = mixed + cand_v[user, :, ncols].astype(F32)
            slot = slot0 + lax.broadcasted_iota(jnp.int32, (384, 256), 0)
            out_v[user, :, ncols] = jnp.where(slot < ccount_ref[user], mixed, 0.0).astype(BF16)
            if user == 0:
                for piece in range(3):
                    norm(1, pl.ds(n * 96 + piece * 32, 32))
        pltpu.make_async_copy(out_v.at[user], out_ref.at[user], local_sem.at[3 + user]).start()
    for user in range(users_here):
        pltpu.make_async_copy(out_v.at[user], out_ref.at[user], local_sem.at[3 + user]).wait()
    for number in range(HEADS):
        kv_copy(number // 2, number % 2, c).wait_send()
    for src, k in sent:
        rcopy(src, src, k, sib).wait_send()
    assert state["k"] <= NSEM


def body(candidates, history, proj_weight, out_weight, hist_len, cand_count):
    anyspace = pl.BlockSpec(memory_space=pl.ANY)
    smem = pl.BlockSpec(memory_space=pltpu.SMEM)
    vmem = pl.BlockSpec(memory_space=pltpu.VMEM)
    return pl.pallas_call(
        kernel,
        out_shape=jax.ShapeDtypeStruct(candidates.shape, BF16),
        in_specs=[anyspace, anyspace, vmem, anyspace, smem, smem],
        out_specs=anyspace,
        scratch_shapes=[
            pltpu.VMEM((2, NX, NY, NZ, 16, 1024), BF16),
            pltpu.VMEM((NX, 2, 2, 32, 1024), BF16),
            pltpu.VMEM((4, 2, 2, 512, 256), BF16),
            pltpu.VMEM((2, 2, 2, 384, 128), BF16),
            pltpu.VMEM((2, 2, 4, 128, 1024), BF16),
            pltpu.VMEM((256, 256), BF16),
            pltpu.VMEM((2, 384, 1024), BF16),
            pltpu.VMEM((1024, 1024), BF16),
            pltpu.VMEM((512, 128), F32),
            pltpu.VMEM((2, 384, 1024), F32),
            pltpu.VMEM((2, 384, 1024), BF16),
            pltpu.VMEM((2, 384, 1024), BF16),
            pltpu.VMEM((2, 384, 1024), BF16),
            pltpu.SemaphoreType.DMA((NSEM,)),
            pltpu.SemaphoreType.DMA((NSEM,)),
            pltpu.SemaphoreType.DMA((5,)),
        ],
        compiler_params=pltpu.CompilerParams(
            collective_id=0, has_side_effects=True, vmem_limit_bytes=56 * 1024 * 1024
        ),
    )(candidates, history, proj_weight, out_weight, hist_len, cand_count)


def solution(mesh):
    in_specs = (
        P("users", "score", None),
        P("users", "score", None),
        P(("users", "score"), None, None),
        P(),
        P("users"),
        P("users"),
    )
    out_specs = P("users", "score", None)
    return jax.shard_map(body, mesh=mesh, in_specs=in_specs, out_specs=out_specs, check_vma=False)
```

```python
import functools
import math

import jax
import jax.numpy as jnp
from jax import lax
from jax.experimental import pallas as pl
from jax.experimental.pallas import tpu as pltpu
from jax.sharding import PartitionSpec as P

MESH = pl.DeviceIdType.MESH
HEADS = 8
NX, NY, NZ = 4, 4, 8
BF16, F32 = jnp.bfloat16, jnp.float32
COLS_X, COLS_Y, COLS_Z = pl.ds(0, 256), pl.ds(256, 384), pl.ds(640, 384)
COLS_XY = pl.ds(0, 640)
SLOT = {0: 0, -1: 1, 1: 2, -2: 3, 2: 4, -3: 5, 3: 6, 4: 7, -4: 7}
NSEM = 128


def nt_dot(a, b):
    return lax.dot_general(a, b, (((1,), (1,)), ((), ())), preferred_element_type=F32)


def half_silu(t):
    return t + t * jnp.tanh(t)


def kernel(
    cand_ref, hist_ref, proj_ref, ow_ref, hlen_ref, ccount_ref, out_ref,
    G, H, KV, Q, W, pick_v, cand_v, ow_v, mask_v, attn, gate, gated, out_v, send_sem, recv_sem, local_sem,
):
    u = lax.axis_index("users")
    s = lax.axis_index("score")
    z = lax.rem(u, NZ)
    yhi = lax.div(u, NZ)
    c = lax.rem(s, 2)
    x = lax.rem(lax.div(s, 2), NX)
    ylo = lax.div(s, 8)
    y = yhi * 2 + ylo
    oc = 1 - c

    def dev(px, py, pz, pc):
        return (lax.div(py, 2) * NZ + pz, lax.rem(py, 2) * 8 + px * 2 + pc)

    def up(pos, n, k):
        return lax.rem(pos + k + n, n)

    yo = y + 1 - 2 * ylo
    sib = dev(x, y, z, oc)
    local = [
        pltpu.make_async_copy(hist_ref.at[c], H.at[x, ylo, c], local_sem.at[0]),
        pltpu.make_async_copy(cand_ref, cand_v, local_sem.at[1]),
        pltpu.make_async_copy(ow_ref, ow_v, local_sem.at[2]),
    ]
    for copy in local:
        copy.start()

    barrier = pltpu.get_barrier_semaphore()
    partners = [dev(up(x, NX, k), y, z, c) for k in (1, 3, 2)] + [dev(x, up(y, NY, k), z, c) for k in (1, 3, 2)]
    partners += [dev(x, y, up(z, NZ, k), c) for k in (1, 7, 2, 6, 3, 5, 4)] + [sib, dev(x, yo, z, oc)]
    for partner in partners:
        pl.semaphore_signal(barrier, inc=1, device_id=partner, device_id_type=MESH)

    row16 = lax.broadcasted_iota(jnp.int32, (16, 1024), 0)
    tile = jnp.zeros((16, 1024), F32)
    for f in range(4):
        rows_f = proj_ref[f].astype(F32)
        for p in range(4):
            tile = jnp.where(row16 == f * 4 + p, jnp.broadcast_to(rows_f[p : p + 1], (16, 1024)), tile)
    G[c, x, y, 0] = tile.astype(BF16)

    pl.semaphore_wait(barrier, len(partners))

    state = {"k": 0}
    sent = []

    def new_sem():
        k = state["k"]
        state["k"] = k + 1
        return k

    def rcopy(src, dst, k, target):
        return pltpu.make_async_remote_copy(
            src_ref=src(), dst_ref=dst(), send_sem=send_sem.at[k], recv_sem=recv_sem.at[k],
            device_id=target, device_id_type=MESH,
        )

    def send(src, dst, k, target):
        rcopy(src, dst, k, target).start()
        sent.append((src, k))

    def wait(dst, k):
        rcopy(dst, dst, k, sib).wait_recv()

    hist_arrivals = []
    for who, target, py, pc in (
        (oc, sib, ylo, oc), (c, dev(x, yo, z, c), 1 - ylo, c), (oc, dev(x, yo, z, oc), 1 - ylo, oc),
    ):
        k = new_sem()
        send(functools.partial(hist_ref.at.__getitem__, who), lambda: H.at[x, ylo, c], k, target)
        hist_arrivals.append((functools.partial(H.at.__getitem__, (x, py, pc)), k))

    whole = slice(None)

    def view(plane, xs, ys, slots, columns):
        return lambda: G.at[plane, xs, ys, slots, :, columns]

    def direct(axis, block):
        n, at = (NX, x) if axis == "x" else (NY, y)
        arrivals = []
        for step in (1, 3, 2):
            k = new_sem()
            to = up(at, n, step)
            send(block(at), block(at), k, dev(to, y, z, c) if axis == "x" else dev(x, to, z, c))
            arrivals.append((block(up(at, n, -step)), k))
        return arrivals

    def settle(arrivals):
        for where, k in arrivals:
            wait(where, k)

    waves = {2: pl.ds(3, 2), 3: pl.ds(5, 2), 4: pl.ds(7, 1)}
    groups = [pl.ds(0, 3), pl.ds(3, 2), pl.ds(5, 3)]

    def second(w):
        group_x = direct("y", lambda at: view(c, x, at, groups[w], COLS_X))
        group_y = direct("x", lambda at: view(c, at, y, groups[w], COLS_Y))
        return group_x, group_y

    def third(w, arrivals):
        settle(arrivals[0])
        group_x = direct("x", lambda at: view(c, at, whole, groups[w], COLS_X))
        settle(arrivals[1])
        group_y = direct("y", lambda at: view(c, whole, at, groups[w], COLS_Y))
        return group_x + group_y

    spot = {"x": [up(x, NX, k) for k in range(NX)], "y": [up(y, NY, k) for k in range(NY)]}
    neighbour = {
        "x": [dev(spot["x"][k], y, z, c) for k in range(NX)],
        "y": [dev(x, spot["y"][k], z, c) for k in range(NY)],
    }

    def ring_plan(axis, block):
        first = [(block(spot[axis][3], None), new_sem()), (block(spot[axis][1], None), new_sem())]
        return first, [(block(spot[axis][2], half), new_sem()) for half in range(2)]

    def ring_first(axis, block, plan):
        for (_, k), step in zip(plan[0], (1, 3)):
            send(block(spot[axis][0], None), block(spot[axis][0], None), k, neighbour[axis][step])

    def ring_second(axis, block, plan):
        settle(plan[0])
        for half, step in ((0, 1), (1, 3)):
            mine = block(spot[axis][4 - step], half)
            send(mine, mine, plan[1][half][1], neighbour[axis][step])

    def hist_block(at, half):
        return (lambda: H.at[at]) if half is None else (lambda: H.at[at, half])

    hist_plan = ring_plan("x", hist_block)
    along_z = {}

    def z_send(off):
        k = new_sem()
        send(view(c, x, y, 0, COLS_XY), view(c, x, y, SLOT[-off], COLS_XY), k, dev(x, y, up(z, NZ, off), c))
        along_z[SLOT[-off]] = (view(c, x, y, SLOT[-off], COLS_XY), k)

    zx = direct("x", lambda at: view(c, at, y, 0, COLS_Z))
    for off in (1, -1, 2, -2, 3, -3, 4):
        z_send(off)
    settle([along_z[1], along_z[2]])
    stage2 = {0: second(0)}
    local[0].wait()
    settle(hist_arrivals)
    ring_first("x", hist_block, hist_plan)
    settle(zx)
    zy = direct("y", lambda at: view(c, whole, at, 0, COLS_Z))
    settle([along_z[3], along_z[4]])
    stage2[1] = second(1)
    settle(zy)

    z_right, z_left = dev(x, y, up(z, NZ, 1), c), dev(x, y, up(z, NZ, -1), c)
    ring_sems = [(new_sem(), new_sem()) for _ in range(4)]
    first_xy, first_z = new_sem(), new_sem()
    twin_sems = {w: new_sem() for w in (2, 3, 4)}
    kv_sems = [new_sem() for _ in range(HEADS)]

    def ring_blocks(w):
        xs = (whole, whole) if w < 4 else (pl.ds(0, 2), pl.ds(2, 2))
        down, high = (2 * w - 3, 2 * w - 2) if w > 1 else (0, 0)
        into = (2 * w - 1, 2 * w) if w < 4 else (7, 7)
        return [
            (view(c, xs[0], whole, down, COLS_Z), view(c, xs[0], whole, into[0], COLS_Z)),
            (view(c, xs[1], whole, high, COLS_Z), view(c, xs[1], whole, into[1], COLS_Z)),
        ]

    def ring_send(w):
        for (src, dst), k, target in zip(ring_blocks(w), ring_sems[w - 1], (z_right, z_left)):
            send(src, dst, k, target)

    def ring_wait(w):
        for (_, dst), k in zip(ring_blocks(w), ring_sems[w - 1]):
            wait(dst, k)

    def twin_send(w):
        block = view(c, whole, whole, waves[w], whole)
        send(block, block, twin_sems[w], sib)

    def twin_wait(w):
        wait(view(oc, whole, whole, waves[w], whole), twin_sems[w])

    ring_send(1)
    stage3 = third(0, stage2[0])
    settle([along_z[5], along_z[6], along_z[7]])
    stage2[2] = second(2)
    ring_wait(1)
    ring_send(2)
    block = view(c, whole, whole, groups[0], COLS_Z)
    send(block, block, first_z, sib)
    ring_second("x", hist_block, hist_plan)
    later = {1: third(1, stage2[1])}
    settle(stage3)
    block_xy = view(c, whole, whole, groups[0], COLS_XY)
    send(block_xy, block_xy, first_xy, sib)
    later[2] = third(2, stage2[2])
    local[1].wait()
    local[2].wait()
    wait(view(oc, whole, whole, groups[0], COLS_Z), first_z)
    wait(view(oc, whole, whole, groups[0], COLS_XY), first_xy)

    head_size = 128
    score_half = 0.5 / math.sqrt(head_size)
    users_here = cand_v.shape[0]

    q = lax.broadcasted_iota(jnp.int32, (512, 128), 0)
    event = (((q >> 6) & 1) * 8 + (q >> 7) * 2 + ((q >> 5) & 1)) * 32 + (q & 31)
    mask_v[...] = (event < hlen_ref[c]).astype(F32)
    out_row = lax.broadcasted_iota(jnp.int32, (256, 256), 0)
    in_row = lax.broadcasted_iota(jnp.int32, (256, 256), 1)
    source = ((out_row & 63) >> 2) * 16 + (out_row & 3) * 4 + (out_row >> 6)
    pick_v[...] = (in_row == source).astype(F32).astype(BF16)

    odd = lax.rem(z, 2)

    def slabs(hi, slot):
        return jnp.concatenate(
            [G[plane, px, hi * 2 + yl, slot] for yl in range(2) for px in range(NX) for plane in range(2)],
            axis=0,
        )

    def choose(t, even_slots, odd_slots):
        slot = jnp.int32(0)
        for number in range(4):
            slot = jnp.where(t == number, jnp.where(odd == 1, odd_slots[number], even_slots[number]), slot)
        return slot

    def pair_of(t):
        turn = t + lax.div(t, 2) - 2 * lax.div(t, 3)
        return lax.rem(lax.div(z, 2) + (2 * odd - 1) * turn + 8, 4)

    def columns_of(t, hi):
        return pl.ds(pl.multiple_of((hi * 4 + pair_of(t)) * 128, 128), 128)

    def project(t, hi):
        slots = (choose(t, (0, 3, 4, 7), (1, 2, 5, 6)), choose(t, (2, 1, 6, 5), (0, 4, 3, 7)))
        keep, at = lax.rem(t, 2), columns_of(t, hi)
        for zl in range(2):
            sorted_rows = jnp.dot(pick_v[...], slabs(hi, slots[zl]), preferred_element_type=F32).astype(BF16)
            for p in range(4):
                W[keep, hi, p, zl * 64 : zl * 64 + 64] = sorted_rows[p * 64 : p * 64 + 64]
        parts = half_silu(0.5 * nt_dot(cand_v[...].reshape(768, 1024), W[keep, hi].reshape(512, 1024))).astype(BF16)
        own_keys, own_values = parts[:, :128], parts[:, 128:256]
        queries, user_gate = parts[:, 256:384], parts[:, 384:]
        own = jnp.dot(queries * own_keys, jnp.ones((128, 128), BF16), preferred_element_type=F32)
        own = half_silu(own * score_half) * own_values.astype(F32)
        for user in range(users_here):
            rows_u = slice(user * 384, user * 384 + 384)
            Q[keep, hi, user] = queries[rows_u]
            gate[user, :, at] = user_gate[rows_u]
            attn[user, :, at] = own[rows_u]

    def keys_values(t, hi):
        w_kv = W[lax.rem(t, 2), hi, 0:2].reshape(256, 1024)
        kv = half_silu(0.5 * nt_dot(H[...].reshape(512, 1024), w_kv))
        KV[t, hi, c, :, :128] = kv[:, :128].astype(BF16)
        KV[t, hi, c, :, 128:] = (kv[:, 128:] * mask_v[...]).astype(BF16)
        kv_copy(t, hi, c).start()

    def attend(t, hi, user):
        keep, at = lax.rem(t, 2), columns_of(t, hi)
        keys, values = KV[t, hi, user, :, :128], KV[t, hi, user, :, 128:]
        weights = half_silu(nt_dot(Q[keep, hi, user], keys) * score_half).astype(BF16)
        attn[user, :, at] += jnp.dot(weights, values, preferred_element_type=F32)

    def both(work, t):
        for hi in range(2):
            work(t, hi)

    def chunk(t, carry):
        @pl.when(t == 1)
        def _():
            settle(hist_plan[1])

        @pl.when(t > 0)
        def _():
            both(keys_values, t - 1)
            both(functools.partial(attend, user=c), t - 1)
            for hi in range(2):
                kv_copy(t - 1, hi, oc).wait_recv()
            both(functools.partial(attend, user=oc), t - 1)

        for w in (2, 3, 4):
            @pl.when(t == w - 1)
            def _():
                twin_wait(w)

        @pl.when(t < 4)
        def _():
            both(project, t)

        def forward(w):
            ring_wait(w)
            if w < 4:
                ring_send(w + 1)
            if w < 4:
                settle(later[w - 1])
            twin_send(w)

        for w in (2, 3, 4):
            @pl.when(t == w - 2)
            def _():
                forward(w)

        return carry

    def kv_copy(t, hi, whose):
        k = kv_sems[0] + t * 2 + hi
        return pltpu.make_async_remote_copy(
            src_ref=KV.at[t, hi, whose], dst_ref=KV.at[t, hi, whose],
            send_sem=send_sem.at[k], recv_sem=recv_sem.at[k], device_id=sib, device_id_type=MESH,
        )

    lax.fori_loop(0, HEADS // 2 + 1, chunk, 0)

    slot0 = s * 384

    def norm(user, block):
        rows_a = attn[user, block]
        mean = jnp.sum(rows_a, axis=1, keepdims=True) * (1.0 / 1024)
        centered = rows_a - mean
        var = jnp.sum(centered * centered, axis=1, keepdims=True) * (1.0 / 1024)
        normed = centered * lax.rsqrt(var + 1e-06)
        gated[user, block] = (normed * gate[user, block].astype(F32)).astype(BF16)

    def norm_step(i, carry):
        norm(0, pl.ds(pl.multiple_of(i * 64, 64), 64))
        return carry

    lax.fori_loop(0, 6, norm_step, 0)
    for user in range(users_here):
        for n in range(4):
            ncols = pl.ds(n * 256, 256)
            mixed = jnp.dot(gated[user], ow_v[:, ncols], preferred_element_type=F32)
            mixed = mixed + cand_v[user, :, ncols].astype(F32)
            slot = slot0 + lax.broadcasted_iota(jnp.int32, (384, 256), 0)
            out_v[user, :, ncols] = jnp.where(slot < ccount_ref[user], mixed, 0.0).astype(BF16)
            if user == 0:
                for piece in range(3):
                    norm(1, pl.ds(n * 96 + piece * 32, 32))
        pltpu.make_async_copy(out_v.at[user], out_ref.at[user], local_sem.at[3 + user]).start()
    for user in range(users_here):
        pltpu.make_async_copy(out_v.at[user], out_ref.at[user], local_sem.at[3 + user]).wait()
    for number in range(HEADS):
        kv_copy(number // 2, number % 2, c).wait_send()
    for src, k in sent:
        rcopy(src, src, k, sib).wait_send()
    assert state["k"] <= NSEM


def body(candidates, history, proj_weight, out_weight, hist_len, cand_count):
    anyspace = pl.BlockSpec(memory_space=pl.ANY)
    smem = pl.BlockSpec(memory_space=pltpu.SMEM)
    vmem = pl.BlockSpec(memory_space=pltpu.VMEM)
    return pl.pallas_call(
        kernel,
        out_shape=jax.ShapeDtypeStruct(candidates.shape, BF16),
        in_specs=[anyspace, anyspace, vmem, anyspace, smem, smem],
        out_specs=anyspace,
        scratch_shapes=[
            pltpu.VMEM((2, NX, NY, NZ, 16, 1024), BF16),
            pltpu.VMEM((NX, 2, 2, 32, 1024), BF16),
            pltpu.VMEM((4, 2, 2, 512, 256), BF16),
            pltpu.VMEM((2, 2, 2, 384, 128), BF16),
            pltpu.VMEM((2, 2, 4, 128, 1024), BF16),
            pltpu.VMEM((256, 256), BF16),
            pltpu.VMEM((2, 384, 1024), BF16),
            pltpu.VMEM((1024, 1024), BF16),
            pltpu.VMEM((512, 128), F32),
            pltpu.VMEM((2, 384, 1024), F32),
            pltpu.VMEM((2, 384, 1024), BF16),
            pltpu.VMEM((2, 384, 1024), BF16),
            pltpu.VMEM((2, 384, 1024), BF16),
            pltpu.SemaphoreType.DMA((NSEM,)),
            pltpu.SemaphoreType.DMA((NSEM,)),
            pltpu.SemaphoreType.DMA((5,)),
        ],
        compiler_params=pltpu.CompilerParams(
            collective_id=0, has_side_effects=True, vmem_limit_bytes=56 * 1024 * 1024
        ),
    )(candidates, history, proj_weight, out_weight, hist_len, cand_count)


def solution(mesh):
    in_specs = (
        P("users", "score", None),
        P("users", "score", None),
        P(("users", "score"), None, None),
        P(),
        P("users"),
        P("users"),
    )
    out_specs = P("users", "score", None)
    return jax.shard_map(body, mesh=mesh, in_specs=in_specs, out_specs=out_specs, check_vma=False)
```
